256 devices in a mesh: dp: 32 (over z, x_lo, core), fsdp: 8 (over y, x_hi).
Axes of the slice: x: 4 (x_hi: 2, x_lo: 2; x = x_hi * 2 + x_lo), y: 4, z: 8, core: 2. Of those that a mesh axis runs over, the one named last changes fastest.
Arguments:
- inputs: bfloat16 [1024, 256, 512], P(('dp', 'fsdp')), may hold values from -0.25 to 0.25
- out_grad: bfloat16 [1024, 256, 512], P(('dp', 'fsdp')), may hold values from -6 to 6
- coeff_fixed: int32 [1024, 16], P(('dp', 'fsdp')), may hold values from 0 to 4096
- atom_counts: int32 [1024], P(('dp', 'fsdp')), may hold values from 64 to 256, as said below
- experts: bfloat16 [16, 512, 512], P(None, ('dp', 'fsdp')), may hold values from -0.125 to 0.125
Outputs:
- in_grad: bfloat16 [1024, 256, 512], P(('dp', 'fsdp'))
- expert_grad: float32 [16, 512, 512], P(None, ('dp', 'fsdp'))
The draws below stay inside these ranges and needn't reach their ends.
Inputs may be any that keep to these rules, and one draw needn't show every extreme that they name: `atom_counts`: some system has exactly 256 atoms and some exactly 64.
All inputs are finite; a program needn't handle non-finite values.
Results may differ from the reference program's by a relative error of at most 0.0049.
Values may be sent and summed in bfloat16 or wider, within the bound.
No kernel may reach another device: no remote copies, remote signals or barrier semaphores. Data moves between devices by JAX's collectives and lax.ppermute only.
A program may use at most 128 MiB of HBM per device.

```python
import jax
import jax.numpy as jnp
from jax import lax

D = 512
EXPERTS = 16
SYS_DEV = 4
MAX_ATOMS = 256
SYSTEMS = 1024


def draw_atom_counts(key, part):
    first = jax.random.fold_in(key, 11)
    second = jax.random.fold_in(key, 12)
    counts = jax.random.randint(first, (SYSTEMS,), MAX_ATOMS // 4, MAX_ATOMS + 1, dtype=jnp.int32)
    where = jax.random.randint(second, (), 0, SYSTEMS, dtype=jnp.int32)
    counts = counts.at[where].set(MAX_ATOMS)
    counts = counts.at[(where + 1) % SYSTEMS].set(MAX_ATOMS // 4)
    return counts


def touch_ends(array, rng, smallest, largest):
    dims = array.shape
    place = [jax.random.randint(jax.random.fold_in(rng, axis), (), 0, dims[axis]) for axis in range(len(dims))]
    array = array.at[tuple(place)].set(smallest)
    longest = dims.index(max(dims))
    place[longest] = (place[longest] + 1) % dims[longest]
    return array.at[tuple(place)].set(largest)


def spiked(result, own_key, source, target, blocks, factor):
    owner, partner = [(jnp.arange(result.shape[dim]) // (result.shape[dim] // blocks)).reshape([-1 if axis == dim else 1 for axis in range(result.ndim)]) for dim in (source, target)]
    chosen = jax.random.permutation(own_key, blocks)[partner]
    strong = (owner == chosen) | (owner == (partner + blocks // 2) % blocks)
    return jnp.where(strong, factor * result, result)


def shard_levels(rng, dims, cuts, low, top_value):
    gain, own = 1.0, jax.random.fold_in(rng, 6)
    for position, shards_of in cuts:
        draws = jnp.exp(jax.random.uniform(jax.random.fold_in(own, position), (shards_of,), jnp.float32, low / len(cuts), top_value / len(cuts)))
        gain = gain * jnp.repeat(draws, dims[position] // shards_of).reshape([-1 if axis == position else 1 for axis in range(len(dims))])
    return gain


def noise(stream_key, shape, deviation, most, split=(), kind=jnp.bfloat16):
    array = deviation * jax.random.normal(stream_key, shape, jnp.float32)
    if split:
        array = array * shard_levels(stream_key, shape, split, -0.22, 0.18)
    return jnp.clip(array, -most, most).astype(kind)


def heavy_noise(own_key, dims, scale, reach, split, heavy, held_as=jnp.bfloat16):
    entries = scale * jax.random.normal(own_key, dims, jnp.float32)
    if split:
        entries = entries * shard_levels(own_key, dims, split, -0.22, 0.18)
    return jnp.clip(spiked(entries, jax.random.fold_in(own_key, 3), *heavy), -reach, reach).astype(held_as)


def setup_inputs(seed: int = 0) -> dict:
    streams_of = jax.random.split(jax.random.key(seed), 6)
    inputs = heavy_noise(streams_of[0], (SYSTEMS, MAX_ATOMS, D), (2.0 / (SYSTEMS * MAX_ATOMS) ** 0.5), 0.25, ((0, 256),), (0, 2, 256, 6.0))
    out_grad = noise(streams_of[1], (SYSTEMS, MAX_ATOMS, D), 1.0, 6.0, ((0, 256),))
    coeff_fixed = touch_ends(jax.random.randint(streams_of[2], (SYSTEMS, EXPERTS), 0, 4097), jax.random.fold_in(streams_of[2], 1), 0, 4096).astype(jnp.int32)
    atom_counts = draw_atom_counts(jax.random.fold_in(streams_of[5], 71), 0)
    experts = noise(streams_of[4], (EXPERTS, D, D), (4 * D) ** -0.5, 0.125, ((1, 256),))
    return dict(inputs=inputs, out_grad=out_grad, coeff_fixed=coeff_fixed, atom_counts=atom_counts, experts=experts)


HIGH = lax.Precision.HIGHEST


def reference(inputs, out_grad, coeff_fixed, atom_counts, experts):
    nsys = inputs.shape[0]
    blocks = nsys // SYS_DEV
    flat_experts = experts.astype(jnp.float32).reshape(EXPERTS, D * D)
    xs = inputs.reshape(blocks, SYS_DEV, MAX_ATOMS, D)
    gs = out_grad.reshape(blocks, SYS_DEV, MAX_ATOMS, D)
    qs = coeff_fixed.reshape(blocks, SYS_DEV, EXPERTS)
    ns = atom_counts.reshape(blocks, SYS_DEV)

    def step(total, block):
        acts, grads, fixed, counts = block
        coeffs = fixed.astype(jnp.float32) / 4096.0
        valid = jnp.arange(MAX_ATOMS, dtype=jnp.int32)[None, :] < counts[:, None]
        masked = jnp.where(valid[:, :, None], grads, jnp.zeros_like(grads)).astype(jnp.float32)
        merged = jnp.dot(coeffs, flat_experts, precision=HIGH).reshape(SYS_DEV, D, D)
        merged = lax.optimization_barrier(merged.astype(jnp.bfloat16)).astype(jnp.float32)
        in_grad = jnp.einsum("smj,sij->smi", masked, merged, precision=HIGH).astype(jnp.bfloat16)
        per_system = jnp.einsum("smi,smj->sij", acts.astype(jnp.float32), masked, precision=HIGH)
        total = total + jnp.einsum("se,sij->eij", coeffs, per_system, precision=HIGH)
        return total, in_grad

    total, in_grads = lax.scan(step, jnp.zeros((EXPERTS, D, D), jnp.float32), (xs, gs, qs, ns))
    return in_grads.reshape(nsys, MAX_ATOMS, D), total
```

```python
import jax
import jax.numpy as jnp
from jax import lax
from jax.experimental import pallas as pl
from jax.experimental.pallas import tpu as pltpu
from jax.sharding import Mesh, PartitionSpec as P

AXES = (("z", 8), ("xl", 2), ("core", 2), ("y", 4), ("xh", 2))
NAMES = tuple(name for name, _ in AXES)
PLANE = ("xl", "core", "y", "xh")
NZ = 8
NG = 32
ROWS = 2
PER = NZ * ROWS
D = 512
E = 16
K = 4
M = 256
F32 = jnp.float32
BF16 = jnp.bfloat16
LIMIT = pltpu.CompilerParams(vmem_limit_bytes=32 * 1024 * 1024)


def order():
    to = lax.broadcasted_iota(jnp.int32, (D, D), 0)
    at = lax.broadcasted_iota(jnp.int32, (D, D), 1)
    g, z, r = to // PER, (to // ROWS) % NZ, to % ROWS
    return jnp.where(z * (NG * ROWS) + g * ROWS + r == at, 1.0, 0.0).astype(BF16)


def matmul(a, b, dims):
    return lax.dot_general(a, b, (dims, ((), ())), preferred_element_type=F32)


def masked_of(grad, count):
    slot = lax.broadcasted_iota(jnp.int32, (M, D), 0)
    return jnp.where(slot < count, grad.astype(F32), 0.0).astype(BF16)


def outer_kernel(counts, x, grad, out, pick):
    k = pl.program_id(0)

    @pl.when(k == 0)
    def _():
        pick[...] = order()

    turned = matmul(pick[...], x[0], ((1,), (1,))).astype(BF16)
    masked = masked_of(grad[0], counts[k])
    product = matmul(turned, masked, ((1,), (0,)))
    out[...] = product.astype(BF16).reshape(NG, 1, PER, D)


def outer(counts, x, grad):
    return pl.pallas_call(
        outer_kernel,
        grid_spec=pltpu.PrefetchScalarGridSpec(
            num_scalar_prefetch=1,
            grid=(K,),
            in_specs=[
                pl.BlockSpec((1, M, D), lambda k, c: (k, 0, 0)),
                pl.BlockSpec((1, M, D), lambda k, c: (k, 0, 0)),
            ],
            out_specs=pl.BlockSpec((NG, 1, PER, D), lambda k, c: (0, k, 0, 0)),
            scratch_shapes=[pltpu.VMEM((D, D), BF16)],
        ),
        out_shape=jax.ShapeDtypeStruct((NG, K, PER, D), BF16),
        compiler_params=LIMIT,
        cost_estimate=pl.CostEstimate(flops=2 * K * D * D * (M + M), bytes_accessed=4 << 20, transcendentals=0),
        name="outer",
    )(counts, x, grad)


def spread(fixed):
    n = fixed.shape[0]
    width = NZ * E * ROWS
    lane = lax.broadcasted_iota(jnp.int32, (E, width), 1)
    row = lax.broadcasted_iota(jnp.int32, (E, width), 0)
    widen = jnp.where((lane // ROWS) % E == row, 1.0, 0.0).astype(BF16)
    q = lax.broadcasted_iota(jnp.int32, (n * PER, width), 0) % PER
    col = lax.broadcasted_iota(jnp.int32, (n * PER, width), 1)
    same = (q // ROWS == col // (E * ROWS)) & (q % ROWS == col % ROWS)
    high = (fixed // 64).astype(F32) * (1.0 / 64.0)
    low = (fixed % 64).astype(F32) * (1.0 / 4096.0)
    parts = []
    for part in (high, low):
        wide = matmul(part.astype(BF16), widen, ((1,), (0,)))
        tall = jnp.broadcast_to(wide[:, None, :], (n, PER, width)).reshape(n * PER, width)
        parts.append(jnp.where(same, tall, 0.0).astype(BF16))
    return parts


STEP = 32


def merge_kernel(fixed, experts, out):
    high, low = spread(fixed[...])
    e = experts[...]
    total = matmul(high, e, ((1,), (0,))) + matmul(low, e, ((1,), (0,)))
    out[...] = total.astype(BF16)


def merge(fixed, experts):
    systems = NG * K
    width = NZ * E * ROWS
    return pl.pallas_call(
        merge_kernel,
        grid=(systems // STEP,),
        in_specs=[
            pl.BlockSpec((STEP, E), lambda s: (s, 0)),
            pl.BlockSpec((width, D), lambda s: (0, 0)),
        ],
        out_specs=pl.BlockSpec((STEP * PER, D), lambda s: (s, 0)),
        out_shape=jax.ShapeDtypeStruct((systems * PER, D), BF16),
        compiler_params=LIMIT,
        cost_estimate=pl.CostEstimate(flops=4 * systems * PER * width * D, bytes_accessed=3 << 20, transcendentals=0),
        name="merge",
    )(fixed, experts)


def mix_kernel(fixed, terms, out):
    high, low = spread(fixed[...])
    t = terms[...]
    total = matmul(high, t, ((0,), (0,))) + matmul(low, t, ((0,), (0,)))

    @pl.when(pl.program_id(0) == 0)
    def _():
        out[...] = total

    @pl.when(pl.program_id(0) > 0)
    def _():
        out[...] += total


def mix(fixed, terms):
    systems = NG * K
    width = NZ * E * ROWS
    return pl.pallas_call(
        mix_kernel,
        grid=(systems // STEP,),
        in_specs=[
            pl.BlockSpec((STEP, E), lambda s: (s, 0)),
            pl.BlockSpec((STEP * PER, D), lambda s: (s, 0)),
        ],
        out_specs=pl.BlockSpec((width, D), lambda s: (0, 0)),
        out_shape=jax.ShapeDtypeStruct((width, D), F32),
        compiler_params=LIMIT,
        cost_estimate=pl.CostEstimate(flops=4 * systems * PER * width * D, bytes_accessed=3 << 20, transcendentals=0),
        name="mix",
    )(fixed, terms)


def back_kernel(counts, grad, merged, out, pick):
    k = pl.program_id(0)

    @pl.when(k == 0)
    def _():
        pick[...] = order()

    masked = masked_of(grad[0], counts[k])
    weights = merged[...].reshape(D, D)
    moved = matmul(masked, weights, ((1,), (1,))).astype(BF16)
    out[0] = matmul(moved, pick[...], ((1,), (0,))).astype(BF16)


def back(counts, grad, merged):
    return pl.pallas_call(
        back_kernel,
        grid_spec=pltpu.PrefetchScalarGridSpec(
            num_scalar_prefetch=1,
            grid=(K,),
            in_specs=[
                pl.BlockSpec((1, M, D), lambda k, c: (k, 0, 0)),
                pl.BlockSpec((NG, 1, PER, D), lambda k, c: (0, k, 0, 0)),
            ],
            out_specs=pl.BlockSpec((1, M, D), lambda k, c: (k, 0, 0)),
            scratch_shapes=[pltpu.VMEM((D, D), BF16)],
        ),
        out_shape=jax.ShapeDtypeStruct((K, M, D), BF16),
        compiler_params=LIMIT,
        cost_estimate=pl.CostEstimate(flops=4 * K * M * D * D, bytes_accessed=4 << 20, transcendentals=0),
        name="back",
    )(counts, grad, merged)


def swap(array, axes):
    return lax.all_to_all(array, axes, 0, 0, tiled=True)


def shards(inputs, out_grad, coeff_fixed, atom_counts, experts):
    fixed = swap(jnp.broadcast_to(coeff_fixed[None], (NG, K, E)), PLANE).reshape(NG * K, E)
    own = experts.reshape(1, E * ROWS, D)
    rows = swap(jnp.broadcast_to(own, (NZ, E * ROWS, D)), ("z",)).reshape(NZ * E * ROWS, D)
    terms = swap(outer(atom_counts, inputs, out_grad), PLANE)
    merged = swap(merge(fixed, rows).reshape(NG, K, PER, D), PLANE)
    summed = mix(fixed, terms.reshape(NG * K * PER, D))
    arrived = swap(summed.reshape(NZ, E * ROWS, D), ("z",))
    in_grad = back(atom_counts, out_grad, merged)
    return in_grad, arrived.sum(axis=0).reshape(E, ROWS, D)


def solution(mesh):
    split = Mesh(mesh.devices.reshape([size for _, size in AXES]), NAMES)
    placed = (
        P(NAMES, None, None),
        P(NAMES, None, None),
        P(NAMES, None),
        P(NAMES),
        P(None, NAMES, None),
    )
    return jax.shard_map(
        shards,
        mesh=split,
        in_specs=placed,
        out_specs=(P(NAMES, None, None), P(None, NAMES, None)),
        check_vma=False,
    )
```

```python
import jax
import jax.numpy as jnp
from jax import lax
from jax.experimental import pallas as pl
from jax.experimental.pallas import tpu as pltpu
from jax.sharding import Mesh, PartitionSpec as P

AXES = (("z", 8), ("xl", 2), ("core", 2), ("y", 4), ("xh", 2))
NAMES = tuple(name for name, _ in AXES)
PLANE = ("xl", "core", "y", "xh")
NZ = 8
NG = 32
ROWS = 2
PER = NZ * ROWS
D = 512
E = 16
K = 4
M = 256
F32 = jnp.float32
BF16 = jnp.bfloat16
LIMIT = pltpu.CompilerParams(vmem_limit_bytes=56 * 1024 * 1024)


def row_of(shape, dim):
    return lax.broadcasted_iota(jnp.int32, shape, dim)


def order():
    to = row_of((D, 1), 0)
    source = (((to >> 1) & (NZ - 1)) << 6) + ((to >> 4) << 1) + (to & 1)
    return jnp.where(source == row_of((1, D), 1), 1.0, 0.0).astype(BF16)


def matmul(a, b, dims):
    return lax.dot_general(a, b, (dims, ((), ())), preferred_element_type=F32)


def masked_of(grad, count):
    return jnp.where(row_of((M, 1), 0) < count, grad, jnp.zeros_like(grad))


def outer_kernel(counts, x, grad, out, pick):
    k = pl.program_id(0)

    @pl.when(k == 0)
    def _():
        pick[...] = order()

    turned = matmul(pick[...], x[0], ((1,), (1,))).astype(BF16)
    masked = masked_of(grad[0], counts[k])
    product = matmul(turned, masked, ((1,), (0,)))
    out[...] = product.astype(BF16).reshape(NG, 1, PER, D)


def outer(counts, x, grad):
    return pl.pallas_call(
        outer_kernel,
        grid_spec=pltpu.PrefetchScalarGridSpec(
            num_scalar_prefetch=1,
            grid=(K,),
            in_specs=[
                pl.BlockSpec((1, M, D), lambda k, c: (k, 0, 0)),
                pl.BlockSpec((1, M, D), lambda k, c: (k, 0, 0)),
            ],
            out_specs=pl.BlockSpec((NG, 1, PER, D), lambda k, c: (0, k, 0, 0)),
            scratch_shapes=[pltpu.VMEM((D, D), BF16)],
        ),
        out_shape=jax.ShapeDtypeStruct((NG, K, PER, D), BF16),
        compiler_params=LIMIT,
        cost_estimate=pl.CostEstimate(flops=2 * K * D * D * (M + M), bytes_accessed=4 << 20, transcendentals=0),
        name="outer",
    )(counts, x, grad)


WIDTH = NZ * E * ROWS
STEP = 32


def spread(fixed, z, away):
    n = fixed.shape[0]
    widen = jnp.where(((row_of((E, WIDTH), 1) >> 1) & (E - 1)) == row_of((E, WIDTH), 0), 1.0, 0.0).astype(BF16)
    row = row_of((n * PER, 1), 0) & (PER - 1)
    col = row_of((1, WIDTH), 1)
    line = (z + away * (col >> 5) + NZ) & (NZ - 1)
    same = row == (line << 1) + (col & 1)
    high = (fixed >> 6).astype(F32) * (1.0 / 64.0)
    low = (fixed & 63).astype(F32) * (1.0 / 4096.0)
    parts = []
    for part in (high, low):
        wide = matmul(part.astype(BF16), widen, ((1,), (0,)))
        tall = jnp.broadcast_to(wide[:, None, :], (n, PER, WIDTH)).reshape(n * PER, WIDTH)
        parts.append(jnp.where(same, tall, 0.0).astype(BF16))
    return parts


def merge_kernel(z, fixed, *refs):
    *blocks, out, whole = refs

    @pl.when(pl.program_id(0) == 0)
    def _():
        for n, block in enumerate(blocks):
            whole[n * E * ROWS : (n + 1) * E * ROWS] = block[...]

    high, low = spread(fixed[...], z[0], -1)
    e = whole[...]
    total = matmul(high, e, ((1,), (0,))) + matmul(low, e, ((1,), (0,)))
    out[...] = total.astype(BF16)


def merge(z, fixed, blocks):
    systems = NG * K
    return pl.pallas_call(
        merge_kernel,
        grid_spec=pltpu.PrefetchScalarGridSpec(
            num_scalar_prefetch=1,
            grid=(systems // STEP,),
            in_specs=[pl.BlockSpec((STEP, E), lambda s, z: (s, 0))]
            + [pl.BlockSpec((E * ROWS, D), lambda s, z: (0, 0))] * NZ,
            out_specs=pl.BlockSpec((STEP * PER, D), lambda s, z: (s, 0)),
            scratch_shapes=[pltpu.VMEM((WIDTH, D), BF16)],
        ),
        out_shape=jax.ShapeDtypeStruct((systems * PER, D), BF16),
        compiler_params=LIMIT,
        cost_estimate=pl.CostEstimate(flops=4 * systems * PER * WIDTH * D, bytes_accessed=3 << 20, transcendentals=0),
        name="merge",
    )(z, fixed, *blocks)


def mix_kernel(z, fixed, terms, *refs):
    *outs, total = refs
    step = pl.program_id(0)
    high, low = spread(fixed[...], z[0], 1)
    t = terms[...]
    part = matmul(high, t, ((0,), (0,))) + matmul(low, t, ((0,), (0,)))

    @pl.when(step == 0)
    def _():
        total[...] = part

    @pl.when(step > 0)
    def _():
        total[...] += part

    @pl.when(step == pl.num_programs(0) - 1)
    def _():
        for n, out in enumerate(outs):
            out[...] = total[n * E * ROWS : (n + 1) * E * ROWS]


def mix(z, fixed, terms):
    systems = NG * K
    return pl.pallas_call(
        mix_kernel,
        grid_spec=pltpu.PrefetchScalarGridSpec(
            num_scalar_prefetch=1,
            grid=(systems // STEP,),
            in_specs=[
                pl.BlockSpec((STEP, E), lambda s, z: (s, 0)),
                pl.BlockSpec((STEP * PER, D), lambda s, z: (s, 0)),
            ],
            out_specs=[pl.BlockSpec((E * ROWS, D), lambda s, z: (0, 0))] * NZ,
            scratch_shapes=[pltpu.VMEM((WIDTH, D), F32)],
        ),
        out_shape=[jax.ShapeDtypeStruct((E * ROWS, D), F32)] * NZ,
        compiler_params=LIMIT,
        cost_estimate=pl.CostEstimate(flops=4 * systems * PER * WIDTH * D, bytes_accessed=3 << 20, transcendentals=0),
        name="mix",
    )(z, fixed, terms)


def back_kernel(counts, grad, merged, *refs):
    *sums, out, expert_grad, pick = refs
    k = pl.program_id(0)

    @pl.when(k == 0)
    def _():
        pick[...] = order()

    masked = masked_of(grad[0], counts[k])
    weights = merged[...].reshape(D, D)
    moved = matmul(masked, weights, ((1,), (1,))).astype(BF16)
    out[0] = matmul(moved, pick[...], ((1,), (0,))).astype(BF16)

    @pl.when(k == K - 1)
    def _():
        total = sums[0][...]
        for part in sums[1:]:
            total += part[...]
        for e in range(E):
            expert_grad[e] = total[ROWS * e : ROWS * (e + 1)]


def back(counts, grad, merged, sums):
    return pl.pallas_call(
        back_kernel,
        grid_spec=pltpu.PrefetchScalarGridSpec(
            num_scalar_prefetch=1,
            grid=(K,),
            in_specs=[
                pl.BlockSpec((1, M, D), lambda k, c: (k, 0, 0)),
                pl.BlockSpec((NG, 1, PER, D), lambda k, c: (0, k, 0, 0)),
            ]
            + [pl.BlockSpec((E * ROWS, D), lambda k, c: (0, 0))] * NZ,
            out_specs=[
                pl.BlockSpec((1, M, D), lambda k, c: (k, 0, 0)),
                pl.BlockSpec((E, ROWS, D), lambda k, c: (0, 0, 0)),
            ],
            scratch_shapes=[pltpu.VMEM((D, D), BF16)],
        ),
        out_shape=[
            jax.ShapeDtypeStruct((K, M, D), BF16),
            jax.ShapeDtypeStruct((E, ROWS, D), F32),
        ],
        compiler_params=LIMIT,
        cost_estimate=pl.CostEstimate(flops=4 * K * M * D * D, bytes_accessed=5 << 20, transcendentals=0),
        name="back",
    )(counts, grad, merged, *sums)


def swap(array, axes):
    return lax.all_to_all(array, axes, 0, 0, tiled=True)


def along_z(array, by):
    return lax.ppermute(array, "z", [(i, (i + by) % NZ) for i in range(NZ)])


def shards(inputs, out_grad, coeff_fixed, atom_counts, experts):
    z = lax.axis_index("z").astype(jnp.int32).reshape(1)
    fixed = swap(jnp.broadcast_to(coeff_fixed[None], (NG, K, E)), PLANE).reshape(NG * K, E)
    own = experts.reshape(E * ROWS, D)
    rows = [own] + [along_z(own, n) for n in range(1, NZ)]
    terms = swap(outer(atom_counts, inputs, out_grad), PLANE)
    merged = swap(merge(z, fixed, rows).reshape(NG, K, PER, D), PLANE)
    mixed = mix(z, fixed, terms.reshape(NG * K * PER, D))
    sums = [mixed[0]] + [along_z(mixed[n], n) for n in range(1, NZ)]
    return tuple(back(atom_counts, out_grad, merged, sums))


def solution(mesh):
    split = Mesh(mesh.devices.reshape([size for _, size in AXES]), NAMES)
    placed = (
        P(NAMES, None, None),
        P(NAMES, None, None),
        P(NAMES, None),
        P(NAMES),
        P(None, NAMES, None),
    )
    return jax.shard_map(
        shards,
        mesh=split,
        in_specs=placed,
        out_specs=(P(NAMES, None, None), P(None, NAMES, None)),
        check_vma=False,
    )
```

```python
import jax
import jax.numpy as jnp
from jax import lax
from jax.experimental import pallas as pl
from jax.experimental.pallas import tpu as pltpu
from jax.sharding import Mesh, PartitionSpec as P

AXES = (("z", 8), ("xl", 2), ("core", 2), ("y", 4), ("xh", 2))
NAMES = tuple(name for name, _ in AXES)
PLANE = ("xl", "y", "xh")
NZ = 8
NP = 16
NC = 2
ROWS = 2
PER = NZ * ROWS
PART = 16 * ROWS
D = 512
E = 16
K = 4
M = 256
MERGE_MIB = 62
MIX_MIB = 40
BACK_MIB = 24
F32 = jnp.float32
BF16 = jnp.bfloat16


def vmem(mib):
    return pltpu.CompilerParams(vmem_limit_bytes=mib * 1024 * 1024)


def row_of(shape, dim):
    return lax.broadcasted_iota(jnp.int32, shape, dim)


def order():
    to = row_of((D, 1), 0)
    line, core, r = (to >> 1) & (NZ - 1), (to >> 4) & 1, to & 1
    source = (line << 6) + ((to >> 8) << 5) + (core << 4) + (((to >> 5) & 7) << 1) + r
    return jnp.where(source == row_of((1, D), 1), 1.0, 0.0).astype(BF16)


def matmul(a, b, dims):
    return lax.dot_general(a, b, (dims, ((), ())), preferred_element_type=F32)


def masked_of(grad, count):
    return jnp.where(row_of((M, 1), 0) < count, grad, jnp.zeros_like(grad))


def outer_kernel(counts, x, grad, out, pick):
    k = pl.program_id(0)

    @pl.when(k == 0)
    def _():
        pick[...] = order()

    turned = matmul(pick[...], x[0], ((1,), (1,))).astype(BF16)
    masked = masked_of(grad[0], counts[k])
    product = matmul(turned, masked, ((1,), (0,)))
    out[...] = product.astype(BF16).reshape(NP, 1, NC, PER, D)


def outer(counts, x, grad):
    return pl.pallas_call(
        outer_kernel,
        grid_spec=pltpu.PrefetchScalarGridSpec(
            num_scalar_prefetch=1,
            grid=(K,),
            in_specs=[
                pl.BlockSpec((1, M, D), lambda k, c: (k, 0, 0)),
                pl.BlockSpec((1, M, D), lambda k, c: (k, 0, 0)),
            ],
            out_specs=pl.BlockSpec((NP, 1, NC, PER, D), lambda k, c: (0, k, 0, 0, 0)),
            scratch_shapes=[pltpu.VMEM((D, D), BF16)],
        ),
        out_shape=jax.ShapeDtypeStruct((NP, K, NC, PER, D), BF16),
        compiler_params=vmem(56),
        cost_estimate=pl.CostEstimate(flops=2 * K * D * D * (M + M), bytes_accessed=4 << 20, transcendentals=0),
        name="outer",
    )(counts, x, grad)


WIDTH = NZ * E * ROWS
CHIPS = 4
STEP = CHIPS * K


def spread(fixed, z, away):
    n = fixed.shape[0]
    widen = jnp.where(((row_of((E, WIDTH), 1) >> 1) & (E - 1)) == row_of((E, WIDTH), 0), 1.0, 0.0).astype(BF16)
    row = row_of((n * PER, 1), 0) & (PER - 1)
    col = row_of((1, WIDTH), 1)
    line = (z + away * (col >> 5) + NZ) & (NZ - 1)
    same = row == (line << 1) + (col & 1)
    high = (fixed >> 6).astype(F32) * (1.0 / 64.0)
    low = (fixed & 63).astype(F32) * (1.0 / 4096.0)
    parts = []
    for part in (high, low):
        wide = matmul(part.astype(BF16), widen, ((1,), (0,)))
        tall = jnp.broadcast_to(wide[:, None, :], (n, PER, WIDTH)).reshape(n * PER, WIDTH)
        parts.append(jnp.where(same, tall, 0.0).astype(BF16))
    return parts


def merge_kernel(at, fixed, *refs):
    *blocks, out, whole = refs
    core = at[1]

    @pl.when(pl.program_id(0) == 0)
    def _():
        for n, block in enumerate(blocks):
            whole[core, n * PART : (n + 1) * PART] = block[0]
            whole[1 - core, n * PART : (n + 1) * PART] = block[1]

    high, low = spread(fixed[...], at[0], -1)
    for c in range(NC):
        e = whole[c]
        total = matmul(high, e, ((1,), (0,))) + matmul(low, e, ((1,), (0,)))
        out[:, :, c] = total.astype(BF16).reshape(CHIPS, K, PER, D)


def merge(at, fixed, blocks):
    return pl.pallas_call(
        merge_kernel,
        grid_spec=pltpu.PrefetchScalarGridSpec(
            num_scalar_prefetch=1,
            grid=(NP // CHIPS,),
            in_specs=[pl.BlockSpec((STEP, E), lambda s, at: (s, 0))]
            + [pl.BlockSpec((NC, PART, D), lambda s, at: (0, 0, 0))] * NZ,
            out_specs=pl.BlockSpec((CHIPS, K, NC, PER, D), lambda s, at: (s, 0, 0, 0, 0)),
            scratch_shapes=[pltpu.VMEM((NC, WIDTH, D), BF16)],
        ),
        out_shape=jax.ShapeDtypeStruct((NP, K, NC, PER, D), BF16),
        compiler_params=vmem(MERGE_MIB),
        cost_estimate=pl.CostEstimate(flops=8 * NP * K * PER * WIDTH * D, bytes_accessed=3 << 20, transcendentals=0),
        name="merge",
    )(at, fixed, *blocks)


def mix_kernel(at, fixed, terms, mine, other, total):
    step = pl.program_id(0)
    high, low = spread(fixed[...], at[0], 1)
    for c in range(NC):
        t = terms[:, :, c].reshape(STEP * PER, D)
        part = matmul(high, t, ((0,), (0,))) + matmul(low, t, ((0,), (0,)))
        total[c] = jnp.where(step == 0, part, total[c] + part)

    @pl.when(step == pl.num_programs(0) - 1)
    def _():
        mine[...] = total[at[1]]
        other[...] = total[1 - at[1]]


def mix(at, fixed, terms):
    return pl.pallas_call(
        mix_kernel,
        grid_spec=pltpu.PrefetchScalarGridSpec(
            num_scalar_prefetch=1,
            grid=(NP // CHIPS,),
            in_specs=[
                pl.BlockSpec((STEP, E), lambda s, at: (s, 0)),
                pl.BlockSpec((CHIPS, K, NC, PER, D), lambda s, at: (s, 0, 0, 0, 0)),
            ],
            out_specs=[pl.BlockSpec((WIDTH, D), lambda s, at: (0, 0))] * 2,
            scratch_shapes=[pltpu.VMEM((NC, WIDTH, D), F32)],
        ),
        out_shape=[jax.ShapeDtypeStruct((WIDTH, D), F32)] * 2,
        compiler_params=vmem(MIX_MIB),
        cost_estimate=pl.CostEstimate(flops=8 * NP * K * PER * WIDTH * D, bytes_accessed=3 << 20, transcendentals=0),
        name="mix",
    )(at, fixed, terms)


def both_kernel(a, b, *outs):
    for n, out in enumerate(outs):
        out[...] = a[n * PART : (n + 1) * PART] + b[n * PART : (n + 1) * PART]


def both(a, b):
    return pl.pallas_call(
        both_kernel,
        out_shape=[jax.ShapeDtypeStruct((PART, D), F32)] * NZ,
        compiler_params=vmem(8),
        cost_estimate=pl.CostEstimate(flops=WIDTH * D, bytes_accessed=12 * WIDTH * D, transcendentals=0),
        name="both",
    )(a, b)


def back_kernel(counts, grad, merged, *refs):
    *sums, out, expert_grad, pick = refs
    k = pl.program_id(0)

    @pl.when(k == 0)
    def _():
        pick[...] = order()

    masked = masked_of(grad[0], counts[k])
    weights = merged[...].reshape(D, D)
    moved = matmul(masked, weights, ((1,), (1,))).astype(BF16)
    out[0] = matmul(moved, pick[...], ((1,), (0,))).astype(BF16)

    @pl.when(k == K - 1)
    def _():
        total = sums[0][...]
        for part in sums[1:]:
            total += part[...]
        for e in range(E):
            expert_grad[e] = total[ROWS * e : ROWS * (e + 1)]


def back(counts, grad, merged, sums):
    return pl.pallas_call(
        back_kernel,
        grid_spec=pltpu.PrefetchScalarGridSpec(
            num_scalar_prefetch=1,
            grid=(K,),
            in_specs=[
                pl.BlockSpec((1, M, D), lambda k, c: (k, 0, 0)),
                pl.BlockSpec((NP, 1, NC, PER, D), lambda k, c: (0, k, 0, 0, 0)),
            ]
            + [pl.BlockSpec((PART, D), lambda k, c: (0, 0))] * NZ,
            out_specs=[
                pl.BlockSpec((1, M, D), lambda k, c: (k, 0, 0)),
                pl.BlockSpec((E, ROWS, D), lambda k, c: (0, 0, 0)),
            ],
            scratch_shapes=[pltpu.VMEM((D, D), BF16)],
        ),
        out_shape=[
            jax.ShapeDtypeStruct((K, M, D), BF16),
            jax.ShapeDtypeStruct((E, ROWS, D), F32),
        ],
        compiler_params=vmem(BACK_MIB),
        cost_estimate=pl.CostEstimate(flops=4 * K * M * D * D, bytes_accessed=5 << 20, transcendentals=0),
        name="back",
    )(counts, grad, merged, *sums)


def swap(array, axes):
    return lax.all_to_all(array, axes, 0, 0, tiled=True)


def along_z(array, by):
    return lax.ppermute(array, "z", [(i, (i + by) % NZ) for i in range(NZ)])


def across(array):
    return lax.ppermute(array, "core", [(0, 1), (1, 0)])


def shards(inputs, out_grad, coeff_fixed, atom_counts, experts):
    at = jnp.stack([lax.axis_index("z"), lax.axis_index("core")]).astype(jnp.int32)
    fixed = swap(jnp.broadcast_to(coeff_fixed[None], (NP, K, E)), PLANE).reshape(NP * K, E)
    own = experts.reshape(PART, D)
    pair = jnp.stack([own, across(own)])
    rows = [pair] + [along_z(pair, n) for n in range(1, NZ)]
    terms = swap(outer(atom_counts, inputs, out_grad), PLANE)
    merged = swap(merge(at, fixed, rows), PLANE)
    mine, other = mix(at, fixed, terms)
    mixed = both(mine, across(other))
    sums = [mixed[0]] + [along_z(mixed[n], n) for n in range(1, NZ)]
    return tuple(back(atom_counts, out_grad, merged, sums))


def solution(mesh):
    split = Mesh(mesh.devices.reshape([size for _, size in AXES]), NAMES)
    placed = (
        P(NAMES, None, None),
        P(NAMES, None, None),
        P(NAMES, None),
        P(NAMES),
        P(None, NAMES, None),
    )
    return jax.shard_map(
        shards,
        mesh=split,
        in_specs=placed,
        out_specs=(P(NAMES, None, None), P(None, NAMES, None)),
        check_vma=False,
    )
```

```python
import jax
import jax.numpy as jnp
from jax import lax
from jax.experimental import pallas as pl
from jax.experimental.pallas import tpu as pltpu
from jax.sharding import Mesh, PartitionSpec as P

AXES = (("z", 8), ("xl", 2), ("core", 2), ("y", 4), ("xh", 2))
NAMES = tuple(name for name, _ in AXES)
PLANE = ("xl", "core", "y", "xh")
NZ = 8
NG = 32
ROWS = 2
PER = NZ * ROWS
D = 512
E = 16
K = 4
M = 256
STACK_MIB = 62
MERGE_MIB = 60
MIX_MIB = 56
BACK_MIB = 24
F32 = jnp.float32
BF16 = jnp.bfloat16
LANES = 128
TILES = D // LANES
PART = E * ROWS
WIDTH = NZ * PART
CARD = K * TILES
GROUP = 8
STEP = GROUP * K


def vmem(mib):
    return pltpu.CompilerParams(vmem_limit_bytes=mib * 1024 * 1024)


def row_of(shape, dim):
    return lax.broadcasted_iota(jnp.int32, shape, dim)


def order():
    to = row_of((D, 1), 0)
    source = (((to >> 1) & (NZ - 1)) << 6) + ((to >> 4) << 1) + (to & 1)
    return jnp.where(source == row_of((1, D), 1), 1.0, 0.0).astype(BF16)


def matmul(a, b, dims):
    return lax.dot_general(a, b, (dims, ((), ())), preferred_element_type=F32)


def masked_of(grad, count):
    return jnp.where(row_of((M, 1), 0) < count, grad, jnp.zeros_like(grad))


def card(fixed):
    lane = row_of((E, LANES), 1)
    row = row_of((E, LANES), 0)
    high = (fixed >> 6).astype(F32) * (1.0 / 64.0)
    low = (fixed & 63).astype(F32) * (1.0 / 4096.0)
    first = jnp.where(lane == row, 1.0, 0.0).astype(BF16)
    second = jnp.where(lane == row + E, 1.0, 0.0).astype(BF16)
    return matmul(high.astype(BF16), first, ((1,), (0,))) + matmul(low.astype(BF16), second, ((1,), (0,)))


def outer_kernel(counts, fixed, x, grad, out, pick, held, sheet, sem):
    k = pl.program_id(0)

    def copy(step):
        return pltpu.make_async_copy(
            held.at[:, pl.ds(step * TILES, TILES)], out.at[:, pl.ds(step * TILES, TILES)], sem.at[step]
        )

    def copy_card():
        return pltpu.make_async_copy(held.at[:, pl.ds(CARD, 1)], out.at[:, pl.ds(CARD, 1)], sem.at[K])

    @pl.when(k == 0)
    def _():
        pick[...] = order()
        sheet[...] = jnp.zeros_like(sheet)
        sheet[0:K] = card(fixed[...])
        held[:, CARD] = jnp.broadcast_to(sheet[...].astype(BF16)[None], (NG, PER, LANES))
        copy_card().start()

    turned = matmul(pick[...], x[0], ((1,), (1,))).astype(BF16)
    masked = masked_of(grad[0], counts[k])
    product = matmul(turned, masked, ((1,), (0,))).astype(BF16)
    for tile in range(TILES):
        part = product[:, tile * LANES : (tile + 1) * LANES]
        held[:, k * TILES + tile] = part.reshape(NG, PER, LANES)
    copy(k).start()

    @pl.when(k == K - 1)
    def _():
        copy_card().wait()
        for step in range(K):
            copy(step).wait()


def outer(counts, fixed, x, grad):
    return pl.pallas_call(
        outer_kernel,
        grid_spec=pltpu.PrefetchScalarGridSpec(
            num_scalar_prefetch=1,
            grid=(K,),
            in_specs=[
                pl.BlockSpec((K, E), lambda k, c: (0, 0)),
                pl.BlockSpec((1, M, D), lambda k, c: (k, 0, 0)),
                pl.BlockSpec((1, M, D), lambda k, c: (k, 0, 0)),
            ],
            out_specs=pl.BlockSpec(memory_space=pl.ANY),
            scratch_shapes=[
                pltpu.VMEM((D, D), BF16),
                pltpu.VMEM((NG, CARD + 1, PER, LANES), BF16),
                pltpu.VMEM((PER, LANES), F32),
                pltpu.SemaphoreType.DMA((K + 1,)),
            ],
        ),
        out_shape=jax.ShapeDtypeStruct((NG, CARD + 1, PER, LANES), BF16),
        compiler_params=vmem(56),
        cost_estimate=pl.CostEstimate(flops=2 * K * D * D * (M + M), bytes_accessed=4 << 20, transcendentals=0),
        name="outer",
    )(counts, fixed, x, grad)


def spread(cards, system, z, away):
    chosen = jnp.where(system(row_of((STEP, 1), 0)) == row_of((1, GROUP * PER), 1), 1.0, 0.0).astype(BF16)
    values = matmul(chosen, cards, ((1,), (0,))).astype(BF16)
    lane = row_of((LANES, 2 * WIDTH), 0)
    col = row_of((LANES, 2 * WIDTH), 1)
    widen = jnp.where(lane == ((col >> 1) & (E - 1)) + (col // WIDTH) * E, 1.0, 0.0).astype(BF16)
    wide = matmul(values, widen, ((1,), (0,)))
    row = row_of((STEP * PER, 1), 0) & (PER - 1)
    place = row_of((1, 2 * WIDTH), 1)
    line = (z + away * ((place & (WIDTH - 1)) >> 5) + NZ) & (NZ - 1)
    same = row == (line << 1) + (place & 1)
    tall = jnp.broadcast_to(wide[:, None, :], (STEP, PER, 2 * WIDTH)).reshape(STEP * PER, 2 * WIDTH)
    return jnp.where(same, tall, 0.0).astype(BF16)


def stack_kernel(*refs):
    *blocks, out = refs
    for n, block in enumerate(blocks):
        for half in (0, WIDTH):
            out[half + n * PART : half + (n + 1) * PART] = block[...]


def stack(blocks):
    return pl.pallas_call(
        stack_kernel,
        out_shape=jax.ShapeDtypeStruct((2 * WIDTH, D), BF16),
        compiler_params=vmem(STACK_MIB),
        cost_estimate=pl.CostEstimate(flops=0, bytes_accessed=6 * WIDTH * D, transcendentals=0),
        name="stack",
    )(*blocks)


def merge_kernel(z, cards, rows, out):
    tiles = cards[...].reshape(GROUP * PER, LANES)
    factor = spread(tiles, lambda s: ((s >> 2) << 4) + (s & 3), z[0], -1)
    out[...] = matmul(factor, rows[...], ((1,), (0,))).astype(BF16).reshape(GROUP, K, PER, D)


def merge(z, message, rows):
    return pl.pallas_call(
        merge_kernel,
        grid_spec=pltpu.PrefetchScalarGridSpec(
            num_scalar_prefetch=1,
            grid=(NG // GROUP,),
            in_specs=[
                pl.BlockSpec((GROUP, 1, PER, LANES), lambda s, z: (s, CARD, 0, 0)),
                pl.BlockSpec((2 * WIDTH, D), lambda s, z: (0, 0)),
            ],
            out_specs=pl.BlockSpec((GROUP, K, PER, D), lambda s, z: (s, 0, 0, 0)),
        ),
        out_shape=jax.ShapeDtypeStruct((NG, K, PER, D), BF16),
        compiler_params=vmem(MERGE_MIB),
        cost_estimate=pl.CostEstimate(flops=4 * NG * K * PER * WIDTH * D, bytes_accessed=3 << 20, transcendentals=0),
        name="merge",
    )(z, message, rows)


def mix_kernel(z, message, *refs):
    *outs, total = refs
    step = pl.program_id(0)
    tiles = message[:, CARD].reshape(GROUP * PER, LANES)
    factor = spread(tiles, lambda s: ((s & (GROUP - 1)) << 4) + (s >> 3), z[0], 1)
    columns = []
    for tile in range(TILES):
        parts = [message[:, k * TILES + tile].reshape(GROUP * PER, LANES) for k in range(K)]
        columns.append(jnp.concatenate(parts, axis=0))
    terms = jnp.concatenate(columns, axis=1)
    both = matmul(factor, terms, ((0,), (0,)))
    part = both[:WIDTH] + both[WIDTH:]

    @pl.when(step == 0)
    def _():
        total[...] = part

    @pl.when(step > 0)
    def _():
        total[...] += part

    @pl.when(step == pl.num_programs(0) - 1)
    def _():
        for n, out in enumerate(outs):
            out[...] = total[n * PART : (n + 1) * PART]


def mix(z, message):
    return pl.pallas_call(
        mix_kernel,
        grid_spec=pltpu.PrefetchScalarGridSpec(
            num_scalar_prefetch=1,
            grid=(NG // GROUP,),
            in_specs=[pl.BlockSpec((GROUP, CARD + 1, PER, LANES), lambda s, z: (s, 0, 0, 0))],
            out_specs=[pl.BlockSpec((PART, D), lambda s, z: (0, 0))] * NZ,
            scratch_shapes=[pltpu.VMEM((WIDTH, D), F32)],
        ),
        out_shape=[jax.ShapeDtypeStruct((PART, D), F32)] * NZ,
        compiler_params=vmem(MIX_MIB),
        cost_estimate=pl.CostEstimate(flops=4 * NG * K * PER * WIDTH * D, bytes_accessed=3 << 20, transcendentals=0),
        name="mix",
    )(z, message)


def total_kernel(*refs):
    *sums, out = refs
    total = sums[0][...]
    for part in sums[1:]:
        total += part[...]
    for e in range(E):
        out[e] = total[ROWS * e : ROWS * (e + 1)]


def total(sums):
    return pl.pallas_call(
        total_kernel,
        out_shape=jax.ShapeDtypeStruct((E, ROWS, D), F32),
        compiler_params=vmem(8),
        cost_estimate=pl.CostEstimate(flops=WIDTH * D, bytes_accessed=5 * WIDTH * D, transcendentals=0),
        name="total",
    )(*sums)


def back_kernel(counts, grad, merged, out, pick):
    k = pl.program_id(0)

    @pl.when(k == 0)
    def _():
        pick[...] = order()

    masked = masked_of(grad[0], counts[k])
    weights = merged[...].reshape(D, D)
    moved = matmul(masked, weights, ((1,), (1,))).astype(BF16)
    out[0] = matmul(moved, pick[...], ((1,), (0,))).astype(BF16)


def back(counts, grad, merged):
    return pl.pallas_call(
        back_kernel,
        grid_spec=pltpu.PrefetchScalarGridSpec(
            num_scalar_prefetch=1,
            grid=(K,),
            in_specs=[
                pl.BlockSpec((1, M, D), lambda k, c: (k, 0, 0)),
                pl.BlockSpec((NG, 1, PER, D), lambda k, c: (0, k, 0, 0)),
            ],
            out_specs=pl.BlockSpec((1, M, D), lambda k, c: (k, 0, 0)),
            scratch_shapes=[pltpu.VMEM((D, D), BF16)],
        ),
        out_shape=jax.ShapeDtypeStruct((K, M, D), BF16),
        compiler_params=vmem(BACK_MIB),
        cost_estimate=pl.CostEstimate(flops=4 * K * M * D * D, bytes_accessed=4 << 20, transcendentals=0),
        name="back",
    )(counts, grad, merged)


def swap(array, axes):
    return lax.all_to_all(array, axes, 0, 0, tiled=True)


def along_z(array, by):
    return lax.ppermute(array, "z", [(i, (i + by) % NZ) for i in range(NZ)])


def shards(inputs, out_grad, coeff_fixed, atom_counts, experts):
    z = lax.axis_index("z").astype(jnp.int32).reshape(1)
    message = swap(outer(atom_counts, coeff_fixed, inputs, out_grad), PLANE)
    own = experts.reshape(PART, D)
    rows = stack([own] + [along_z(own, n) for n in range(1, NZ)])
    merged = swap(merge(z, message, rows), PLANE)
    mixed = mix(z, message)
    sums = [mixed[0]] + [along_z(mixed[n], n) for n in range(1, NZ)]
    return back(atom_counts, out_grad, merged), total(sums)


def solution(mesh):
    split = Mesh(mesh.devices.reshape([size for _, size in AXES]), NAMES)
    placed = (
        P(NAMES, None, None),
        P(NAMES, None, None),
        P(NAMES, None),
        P(NAMES),
        P(None, NAMES, None),
    )
    return jax.shard_map(
        shards,
        mesh=split,
        in_specs=placed,
        out_specs=(P(NAMES, None, None), P(None, NAMES, None)),
        check_vma=False,
    )
```

```python
import jax
import jax.numpy as jnp
from jax import lax
from jax.experimental import pallas as pl
from jax.experimental.pallas import tpu as pltpu
from jax.sharding import Mesh, PartitionSpec as P

AXES = (("z", 8), ("xl", 2), ("core", 2), ("y", 4), ("xh", 2))
NAMES = tuple(name for name, _ in AXES)
PLANE = ("xl", "core", "y", "xh")
NZ = 8
NG = 32
ROWS = 2
PER = NZ * ROWS
D = 512
E = 16
K = 4
M = 256
STACK_MIB = 62
MERGE_MIB = 60
MIX_MIB = 56
BACK_MIB = 24
F32 = jnp.float32
BF16 = jnp.bfloat16
LANES = 128
TILES = D // LANES
PART = E * ROWS
WIDTH = NZ * PART
CARD = K * TILES
GROUP = 8
STEP = GROUP * K


def vmem(mib):
    return pltpu.CompilerParams(vmem_limit_bytes=mib * 1024 * 1024)


def row_of(shape, dim):
    return lax.broadcasted_iota(jnp.int32, shape, dim)


def order():
    to = row_of((D, 1), 0)
    source = (((to >> 1) & (NZ - 1)) << 6) + ((to >> 4) << 1) + (to & 1)
    return jnp.where(source == row_of((1, D), 1), 1.0, 0.0).astype(BF16)


def matmul(a, b, dims):
    return lax.dot_general(a, b, (dims, ((), ())), preferred_element_type=F32)


def masked_of(grad, count):
    return jnp.where(row_of((M, 1), 0) < count, grad, jnp.zeros_like(grad))


def card(fixed):
    lane = row_of((E, LANES), 1)
    row = row_of((E, LANES), 0)
    high = (fixed >> 6).astype(F32) * (1.0 / 64.0)
    low = (fixed & 63).astype(F32) * (1.0 / 4096.0)
    first = jnp.where(lane == row, 1.0, 0.0).astype(BF16)
    second = jnp.where(lane == row + E, 1.0, 0.0).astype(BF16)
    return matmul(high.astype(BF16), first, ((1,), (0,))) + matmul(low.astype(BF16), second, ((1,), (0,)))


def outer_kernel(counts, fixed, x, grad, out, xs, grads, pick, held, sheet, ins, outs):
    def fetch(k):
        return (
            pltpu.make_async_copy(x.at[k], xs.at[k], ins.at[2 * k]),
            pltpu.make_async_copy(grad.at[k], grads.at[k], ins.at[2 * k + 1]),
        )

    def send(k):
        place = pl.ds(k * TILES, TILES)
        return pltpu.make_async_copy(held.at[:, place], out.at[:, place], outs.at[k])

    send_card = pltpu.make_async_copy(held.at[:, pl.ds(CARD, 1)], out.at[:, pl.ds(CARD, 1)], outs.at[K])
    fetches = [fetch(k) for k in range(K)]
    for pair in fetches:
        for copy in pair:
            copy.start()
    sheet[...] = jnp.zeros_like(sheet)
    sheet[0:K] = card(fixed[...])
    held[:, CARD] = jnp.broadcast_to(sheet[...].astype(BF16)[None], (NG, PER, LANES))
    send_card.start()
    pick[...] = order()
    for k in range(K):
        fetches[k][0].wait()
        turned = matmul(xs[k], pick[...], ((1,), (1,))).astype(BF16).T
        fetches[k][1].wait()
        product = matmul(turned, masked_of(grads[k], counts[k]), ((1,), (0,))).astype(BF16)
        for tile in range(TILES):
            part = product[:, tile * LANES : (tile + 1) * LANES]
            held[:, k * TILES + tile] = part.reshape(NG, PER, LANES)
        send(k).start()
    send_card.wait()
    for k in range(K):
        send(k).wait()


ANY = pl.BlockSpec(memory_space=pl.ANY)
SCALARS = pl.BlockSpec(memory_space=pltpu.SMEM)
WHOLE = pl.BlockSpec(memory_space=pltpu.VMEM)


def outer(counts, fixed, x, grad):
    return pl.pallas_call(
        outer_kernel,
        in_specs=[SCALARS, WHOLE, ANY, ANY],
        out_specs=ANY,
        scratch_shapes=[
            pltpu.VMEM((K, M, D), BF16),
            pltpu.VMEM((K, M, D), BF16),
            pltpu.VMEM((D, D), BF16),
            pltpu.VMEM((NG, CARD + 1, PER, LANES), BF16),
            pltpu.VMEM((PER, LANES), F32),
            pltpu.SemaphoreType.DMA((2 * K,)),
            pltpu.SemaphoreType.DMA((K + 1,)),
        ],
        out_shape=jax.ShapeDtypeStruct((NG, CARD + 1, PER, LANES), BF16),
        compiler_params=vmem(56),
        cost_estimate=pl.CostEstimate(flops=2 * K * D * D * (M + M), bytes_accessed=4 << 20, transcendentals=0),
        name="outer",
    )(counts, fixed, x, grad)


def one_hot(found):
    return jnp.where(found, 1.0, 0.0).astype(BF16)


def line_of(part, z, away):
    line = (z + away * ((part & (WIDTH - 1)) >> 5) + NZ) & (NZ - 1)
    return (line << 1) + (part & 1)


def source_of(part):
    return ((part >> 1) & (E - 1)) + ((part >> 8) << 4)


def stack_kernel(*refs):
    *blocks, out = refs
    for n, block in enumerate(blocks):
        for half in (0, WIDTH):
            out[half + n * PART : half + (n + 1) * PART] = block[...]


def stack(blocks):
    return pl.pallas_call(
        stack_kernel,
        out_shape=jax.ShapeDtypeStruct((2 * WIDTH, D), BF16),
        compiler_params=vmem(STACK_MIB),
        cost_estimate=pl.CostEstimate(flops=0, bytes_accessed=6 * WIDTH * D, transcendentals=0),
        name="stack",
    )(*blocks)


GROUPS = NG // GROUP
TALL = STEP * PER


def merge_kernel(z, message, rows, out, cards, weights, held, ins, outs):
    fetch_cards = pltpu.make_async_copy(message.at[:, pl.ds(CARD, 1)], cards, ins.at[0])
    fetch_rows = pltpu.make_async_copy(rows, weights, ins.at[1])

    def send(n):
        place = pl.ds(n * GROUP, GROUP)
        return pltpu.make_async_copy(held.at[place], out.at[place], outs.at[n])

    fetch_cards.start()
    fetch_rows.start()
    tall = row_of((TALL, 1), 0)
    pick = one_hot(((tall >> 6) << 4) + ((tall >> 4) & (K - 1)) == row_of((1, GROUP * PER), 1))
    part = row_of((1, 2 * WIDTH), 1)
    widen = one_hot(row_of((LANES, 1), 0) == source_of(part))
    same = (tall & (PER - 1)) == line_of(part, z[0], -1)
    fetch_cards.wait()
    for n in range(GROUPS):
        tiles = cards[n * GROUP : (n + 1) * GROUP].reshape(GROUP * PER, LANES)
        values = matmul(pick, tiles, ((1,), (0,))).astype(BF16)
        factor = jnp.where(same, matmul(values, widen, ((1,), (0,))), 0.0).astype(BF16)
        if n == 0:
            fetch_rows.wait()
        merged = matmul(factor, weights[...], ((1,), (0,))).astype(BF16)
        held[n * GROUP : (n + 1) * GROUP] = merged.reshape(GROUP, K, PER, D)
        send(n).start()
    for n in range(GROUPS):
        send(n).wait()


def merge(z, message, rows):
    return pl.pallas_call(
        merge_kernel,
        in_specs=[SCALARS, ANY, ANY],
        out_specs=ANY,
        scratch_shapes=[
            pltpu.VMEM((NG, 1, PER, LANES), BF16),
            pltpu.VMEM((2 * WIDTH, D), BF16),
            pltpu.VMEM((NG, K, PER, D), BF16),
            pltpu.SemaphoreType.DMA((2,)),
            pltpu.SemaphoreType.DMA((GROUPS,)),
        ],
        out_shape=jax.ShapeDtypeStruct((NG, K, PER, D), BF16),
        compiler_params=vmem(MERGE_MIB),
        cost_estimate=pl.CostEstimate(flops=4 * NG * K * PER * WIDTH * D, bytes_accessed=3 << 20, transcendentals=0),
        name="merge",
    )(z, message, rows)


def mix_kernel(z, message, *refs):
    out, (held, total, ins, outs) = refs[:NZ], refs[NZ:]
    fetches = []
    for n in range(GROUPS):
        place = pl.ds(n * GROUP, GROUP)
        fetches.append(pltpu.make_async_copy(message.at[place], held.at[place], ins.at[n]))
        fetches[n].start()
    tall = row_of((1, TALL), 1)
    pick = one_hot(row_of((GROUP * PER, 1), 0) == (((tall >> 4) & (GROUP - 1)) << 4) + (tall >> 7))
    part = row_of((2 * WIDTH, 1), 0)
    widen = one_hot(source_of(part) == row_of((1, LANES), 1))
    same = line_of(part, z[0], 1) == (tall & (PER - 1))
    for n in range(GROUPS):
        fetches[n].wait()
        place = slice(n * GROUP, (n + 1) * GROUP)
        tiles = held[place, CARD].reshape(GROUP * PER, LANES)
        values = matmul(tiles, pick, ((0,), (0,))).astype(BF16)
        factor = jnp.where(same, matmul(widen, values, ((1,), (0,))), 0.0).astype(BF16)
        columns = []
        for tile in range(TILES):
            pieces = [held[place, k * TILES + tile].reshape(GROUP * PER, LANES) for k in range(K)]
            columns.append(jnp.concatenate(pieces, axis=0))
        both = matmul(factor, jnp.concatenate(columns, axis=1), ((1,), (0,)))
        sums = both[:WIDTH] + both[WIDTH:]
        total[...] = sums if n == 0 else total[...] + sums
    sends = [pltpu.make_async_copy(total.at[pl.ds(n * PART, PART)], out[n], outs.at[n]) for n in range(NZ)]
    for copy in sends:
        copy.start()
    for copy in sends:
        copy.wait()


def mix(z, message):
    return pl.pallas_call(
        mix_kernel,
        in_specs=[SCALARS, ANY],
        out_specs=[ANY] * NZ,
        scratch_shapes=[
            pltpu.VMEM((NG, CARD + 1, PER, LANES), BF16),
            pltpu.VMEM((WIDTH, D), F32),
            pltpu.SemaphoreType.DMA((GROUPS,)),
            pltpu.SemaphoreType.DMA((NZ,)),
        ],
        out_shape=[jax.ShapeDtypeStruct((PART, D), F32)] * NZ,
        compiler_params=vmem(MIX_MIB),
        cost_estimate=pl.CostEstimate(flops=4 * NG * K * PER * WIDTH * D, bytes_accessed=3 << 20, transcendentals=0),
        name="mix",
    )(z, message)


def total_kernel(*refs):
    *sums, out = refs
    total = sums[0][...]
    for part in sums[1:]:
        total += part[...]
    for e in range(E):
        out[e] = total[ROWS * e : ROWS * (e + 1)]


def total(sums):
    return pl.pallas_call(
        total_kernel,
        out_shape=jax.ShapeDtypeStruct((E, ROWS, D), F32),
        compiler_params=vmem(8),
        cost_estimate=pl.CostEstimate(flops=WIDTH * D, bytes_accessed=5 * WIDTH * D, transcendentals=0),
        name="total",
    )(*sums)


def back_kernel(counts, grad, merged, out, pick, held, outs):
    def send(k):
        return pltpu.make_async_copy(held.at[k], out.at[k], outs.at[k])

    pick[...] = order()
    for k in range(K):
        masked = masked_of(grad[k], counts[k])
        moved = matmul(masked, merged[:, k].reshape(D, D), ((1,), (1,))).astype(BF16)
        held[k] = matmul(moved, pick[...], ((1,), (0,))).astype(BF16)
        send(k).start()
    for k in range(K):
        send(k).wait()


def back(counts, grad, merged):
    return pl.pallas_call(
        back_kernel,
        in_specs=[SCALARS, WHOLE, WHOLE],
        out_specs=ANY,
        scratch_shapes=[
            pltpu.VMEM((D, D), BF16),
            pltpu.VMEM((K, M, D), BF16),
            pltpu.SemaphoreType.DMA((K,)),
        ],
        out_shape=jax.ShapeDtypeStruct((K, M, D), BF16),
        compiler_params=vmem(BACK_MIB),
        cost_estimate=pl.CostEstimate(flops=4 * K * M * D * D, bytes_accessed=4 << 20, transcendentals=0),
        name="back",
    )(counts, grad, merged)


def swap(array, axes):
    return lax.all_to_all(array, axes, 0, 0, tiled=True)


def along_z(array, by):
    return lax.ppermute(array, "z", [(i, (i + by) % NZ) for i in range(NZ)])


def shards(inputs, out_grad, coeff_fixed, atom_counts, experts):
    z = lax.axis_index("z").astype(jnp.int32).reshape(1)
    message = swap(outer(atom_counts, coeff_fixed, inputs, out_grad), PLANE)
    own = experts.reshape(PART, D)
    rows = stack([own] + [along_z(own, n) for n in range(1, NZ)])
    merged = swap(merge(z, message, rows), PLANE)
    mixed = mix(z, message)
    sums = [mixed[0]] + [along_z(mixed[n], n) for n in range(1, NZ)]
    return back(atom_counts, out_grad, merged), total(sums)


def solution(mesh):
    split = Mesh(mesh.devices.reshape([size for _, size in AXES]), NAMES)
    placed = (
        P(NAMES, None, None),
        P(NAMES, None, None),
        P(NAMES, None),
        P(NAMES),
        P(None, NAMES, None),
    )
    return jax.shard_map(
        shards,
        mesh=split,
        in_specs=placed,
        out_specs=(P(NAMES, None, None), P(None, NAMES, None)),
        check_vma=False,
    )
```

```python
import jax
import jax.numpy as jnp
from jax import lax
from jax.experimental import pallas as pl
from jax.experimental.pallas import tpu as pltpu
from jax.sharding import Mesh, PartitionSpec as P

AXES = (("z", 8), ("xl", 2), ("core", 2), ("y", 4), ("xh", 2))
NAMES = tuple(name for name, _ in AXES)
PLANE = ("xl", "core", "y", "xh")
NZ = 8
NG = 32
ROWS = 2
PER = NZ * ROWS
D = 512
E = 16
K = 4
M = 256
STACK_MIB = 62
MERGE_MIB = 60
MIX_MIB = 24
BACK_MIB = 24
F32 = jnp.float32
BF16 = jnp.bfloat16
LANES = 128
TILES = D // LANES
PART = E * ROWS
WIDTH = NZ * PART
CARD = K * TILES
GROUP = 8
STEP = GROUP * K


def vmem(mib):
    return pltpu.CompilerParams(vmem_limit_bytes=mib * 1024 * 1024)


def row_of(shape, dim):
    return lax.broadcasted_iota(jnp.int32, shape, dim)


def order():
    to = row_of((D, 1), 0)
    source = (((to >> 1) & (NZ - 1)) << 6) + ((to >> 4) << 1) + (to & 1)
    return jnp.where(source == row_of((1, D), 1), 1.0, 0.0).astype(BF16)


def matmul(a, b, dims):
    return lax.dot_general(a, b, (dims, ((), ())), preferred_element_type=F32)


def masked_of(grad, count):
    return jnp.where(row_of((M, 1), 0) < count, grad, jnp.zeros_like(grad))


def card(fixed):
    lane = row_of((E, LANES), 1)
    row = row_of((E, LANES), 0)
    high = (fixed >> 6).astype(F32) * (1.0 / 64.0)
    low = (fixed & 63).astype(F32) * (1.0 / 4096.0)
    first = jnp.where(lane == row, 1.0, 0.0).astype(BF16)
    second = jnp.where(lane == row + E, 1.0, 0.0).astype(BF16)
    return matmul(high.astype(BF16), first, ((1,), (0,))) + matmul(low.astype(BF16), second, ((1,), (0,)))


def outer_kernel(counts, fixed, x, grad, out, xs, grads, pick, held, sheet, ins, outs):
    def fetch(k):
        return (
            pltpu.make_async_copy(x.at[k], xs.at[k], ins.at[2 * k]),
            pltpu.make_async_copy(grad.at[k], grads.at[k], ins.at[2 * k + 1]),
        )

    def send(k):
        place = pl.ds(k * TILES, TILES)
        return pltpu.make_async_copy(held.at[:, place], out.at[:, place], outs.at[k])

    send_card = pltpu.make_async_copy(held.at[:, pl.ds(CARD, 1)], out.at[:, pl.ds(CARD, 1)], outs.at[K])
    fetches = [fetch(k) for k in range(K)]
    for pair in fetches:
        for copy in pair:
            copy.start()
    sheet[...] = jnp.zeros_like(sheet)
    sheet[0:K] = card(fixed[...])
    held[:, CARD] = jnp.broadcast_to(sheet[...].astype(BF16)[None], (NG, PER, LANES))
    send_card.start()
    pick[...] = order()
    for k in range(K):
        fetches[k][0].wait()
        turned = matmul(xs[k], pick[...], ((1,), (1,))).astype(BF16).T
        fetches[k][1].wait()
        product = matmul(turned, masked_of(grads[k], counts[k]), ((1,), (0,))).astype(BF16)
        for tile in range(TILES):
            part = product[:, tile * LANES : (tile + 1) * LANES]
            held[:, k * TILES + tile] = part.reshape(NG, PER, LANES)
        send(k).start()
    send_card.wait()
    for k in range(K):
        send(k).wait()


ANY = pl.BlockSpec(memory_space=pl.ANY)
SCALARS = pl.BlockSpec(memory_space=pltpu.SMEM)
WHOLE = pl.BlockSpec(memory_space=pltpu.VMEM)


def outer(counts, fixed, x, grad):
    return pl.pallas_call(
        outer_kernel,
        in_specs=[SCALARS, WHOLE, ANY, ANY],
        out_specs=ANY,
        scratch_shapes=[
            pltpu.VMEM((K, M, D), BF16),
            pltpu.VMEM((K, M, D), BF16),
            pltpu.VMEM((D, D), BF16),
            pltpu.VMEM((NG, CARD + 1, PER, LANES), BF16),
            pltpu.VMEM((PER, LANES), F32),
            pltpu.SemaphoreType.DMA((2 * K,)),
            pltpu.SemaphoreType.DMA((K + 1,)),
        ],
        out_shape=jax.ShapeDtypeStruct((NG, CARD + 1, PER, LANES), BF16),
        compiler_params=vmem(56),
        cost_estimate=pl.CostEstimate(flops=2 * K * D * D * (M + M), bytes_accessed=4 << 20, transcendentals=0),
        name="outer",
    )(counts, fixed, x, grad)


def one_hot(found):
    return jnp.where(found, 1.0, 0.0).astype(BF16)


def line_of(part, z, away):
    line = (z + away * ((part & (WIDTH - 1)) >> 5) + NZ) & (NZ - 1)
    return (line << 1) + (part & 1)


def source_of(part):
    return ((part >> 1) & (E - 1)) + ((part >> 8) << 4)


def stack_kernel(*refs):
    *blocks, out = refs
    for n, block in enumerate(blocks):
        for half in (0, WIDTH):
            out[half + n * PART : half + (n + 1) * PART] = block[...]


def stack(blocks):
    return pl.pallas_call(
        stack_kernel,
        out_shape=jax.ShapeDtypeStruct((2 * WIDTH, D), BF16),
        compiler_params=vmem(STACK_MIB),
        cost_estimate=pl.CostEstimate(flops=0, bytes_accessed=6 * WIDTH * D, transcendentals=0),
        name="stack",
    )(*blocks)


GROUPS = NG // GROUP
TALL = STEP * PER


def merge_kernel(z, message, rows, out, cards, weights, held, ins, outs):
    fetch_cards = pltpu.make_async_copy(message.at[:, pl.ds(CARD, 1)], cards, ins.at[0])
    fetch_rows = pltpu.make_async_copy(rows, weights, ins.at[1])

    def send(n):
        place = pl.ds(n * GROUP, GROUP)
        return pltpu.make_async_copy(held.at[place], out.at[place], outs.at[n])

    fetch_cards.start()
    fetch_rows.start()
    tall = row_of((TALL, 1), 0)
    pick = one_hot(((tall >> 6) << 4) + ((tall >> 4) & (K - 1)) == row_of((1, GROUP * PER), 1))
    part = row_of((1, 2 * WIDTH), 1)
    widen = one_hot(row_of((LANES, 1), 0) == source_of(part))
    same = (tall & (PER - 1)) == line_of(part, z[0], -1)
    fetch_cards.wait()
    for n in range(GROUPS):
        tiles = cards[n * GROUP : (n + 1) * GROUP].reshape(GROUP * PER, LANES)
        values = matmul(pick, tiles, ((1,), (0,))).astype(BF16)
        factor = jnp.where(same, matmul(values, widen, ((1,), (0,))), 0.0).astype(BF16)
        if n == 0:
            fetch_rows.wait()
        merged = matmul(factor, weights[...], ((1,), (0,))).astype(BF16)
        held[n * GROUP : (n + 1) * GROUP] = merged.reshape(GROUP, K, PER, D)
        send(n).start()
    for n in range(GROUPS):
        send(n).wait()


def merge(z, message, rows):
    return pl.pallas_call(
        merge_kernel,
        in_specs=[SCALARS, ANY, ANY],
        out_specs=ANY,
        scratch_shapes=[
            pltpu.VMEM((NG, 1, PER, LANES), BF16),
            pltpu.VMEM((2 * WIDTH, D), BF16),
            pltpu.VMEM((NG, K, PER, D), BF16),
            pltpu.SemaphoreType.DMA((2,)),
            pltpu.SemaphoreType.DMA((GROUPS,)),
        ],
        out_shape=jax.ShapeDtypeStruct((NG, K, PER, D), BF16),
        compiler_params=vmem(MERGE_MIB),
        cost_estimate=pl.CostEstimate(flops=4 * NG * K * PER * WIDTH * D, bytes_accessed=3 << 20, transcendentals=0),
        name="merge",
    )(z, message, rows)


def mix_kernel(z, message, *refs):
    out, (held, total, low, ins, outs) = refs[:NZ], refs[NZ:]
    fetches = []
    for n in range(GROUPS):
        place = pl.ds(n * GROUP, GROUP)
        fetches.append(pltpu.make_async_copy(message.at[place], held.at[place], ins.at[n]))
        fetches[n].start()
    tall = row_of((1, TALL), 1)
    pick = one_hot(row_of((GROUP * PER, 1), 0) == (((tall >> 4) & (GROUP - 1)) << 4) + (tall >> 7))
    part = row_of((2 * WIDTH, 1), 0)
    widen = one_hot(source_of(part) == row_of((1, LANES), 1))
    same = line_of(part, z[0], 1) == (tall & (PER - 1))
    for n in range(GROUPS):
        fetches[n].wait()
        place = slice(n * GROUP, (n + 1) * GROUP)
        tiles = held[place, CARD].reshape(GROUP * PER, LANES)
        values = matmul(tiles, pick, ((0,), (0,))).astype(BF16)
        factor = jnp.where(same, matmul(widen, values, ((1,), (0,))), 0.0).astype(BF16)
        columns = []
        for tile in range(TILES):
            pieces = [held[place, k * TILES + tile].reshape(GROUP * PER, LANES) for k in range(K)]
            columns.append(jnp.concatenate(pieces, axis=0))
        both = matmul(factor, jnp.concatenate(columns, axis=1), ((1,), (0,)))
        sums = both[:WIDTH] + both[WIDTH:]
        total[...] = sums if n == 0 else total[...] + sums
    low[...] = total[...].astype(BF16)
    out[0][...] = total[:PART]
    sends = []
    for n in range(1, NZ):
        sends.append(pltpu.make_async_copy(low.at[pl.ds(n * PART, PART)], out[n], outs.at[n - 1]))
    for copy in sends:
        copy.start()
    for copy in sends:
        copy.wait()


def mix(z, message):
    return pl.pallas_call(
        mix_kernel,
        in_specs=[SCALARS, ANY],
        out_specs=[WHOLE] + [ANY] * (NZ - 1),
        scratch_shapes=[
            pltpu.VMEM((NG, CARD + 1, PER, LANES), BF16),
            pltpu.VMEM((WIDTH, D), F32),
            pltpu.VMEM((WIDTH, D), BF16),
            pltpu.SemaphoreType.DMA((GROUPS,)),
            pltpu.SemaphoreType.DMA((NZ - 1,)),
        ],
        out_shape=[jax.ShapeDtypeStruct((PART, D), F32)]
        + [jax.ShapeDtypeStruct((PART, D), BF16)] * (NZ - 1),
        compiler_params=vmem(MIX_MIB),
        cost_estimate=pl.CostEstimate(flops=4 * NG * K * PER * WIDTH * D, bytes_accessed=3 << 20, transcendentals=0),
        name="mix",
    )(z, message)


def total_kernel(own, *refs):
    *sums, out = refs
    total = own[...]
    for part in sums:
        total += part[...].astype(F32)
    for e in range(E):
        out[e] = total[ROWS * e : ROWS * (e + 1)]


def total(own, sums):
    return pl.pallas_call(
        total_kernel,
        out_shape=jax.ShapeDtypeStruct((E, ROWS, D), F32),
        compiler_params=vmem(8),
        cost_estimate=pl.CostEstimate(flops=WIDTH * D, bytes_accessed=5 * WIDTH * D, transcendentals=0),
        name="total",
    )(own, *sums)


def back_kernel(counts, grad, merged, out, pick, held, outs):
    def send(k):
        return pltpu.make_async_copy(held.at[k], out.at[k], outs.at[k])

    pick[...] = order()
    for k in range(K):
        masked = masked_of(grad[k], counts[k])
        moved = matmul(masked, merged[:, k].reshape(D, D), ((1,), (1,))).astype(BF16)
        held[k] = matmul(moved, pick[...], ((1,), (0,))).astype(BF16)
        send(k).start()
    for k in range(K):
        send(k).wait()


def back(counts, grad, merged):
    return pl.pallas_call(
        back_kernel,
        in_specs=[SCALARS, WHOLE, WHOLE],
        out_specs=ANY,
        scratch_shapes=[
            pltpu.VMEM((D, D), BF16),
            pltpu.VMEM((K, M, D), BF16),
            pltpu.SemaphoreType.DMA((K,)),
        ],
        out_shape=jax.ShapeDtypeStruct((K, M, D), BF16),
        compiler_params=vmem(BACK_MIB),
        cost_estimate=pl.CostEstimate(flops=4 * K * M * D * D, bytes_accessed=4 << 20, transcendentals=0),
        name="back",
    )(counts, grad, merged)


def swap(array, axes):
    return lax.all_to_all(array, axes, 0, 0, tiled=True)


def along_z(array, by):
    return lax.ppermute(array, "z", [(i, (i + by) % NZ) for i in range(NZ)])


def shards(inputs, out_grad, coeff_fixed, atom_counts, experts):
    z = lax.axis_index("z").astype(jnp.int32).reshape(1)
    message = swap(outer(atom_counts, coeff_fixed, inputs, out_grad), PLANE)
    own = experts.reshape(PART, D)
    rows = stack([own] + [along_z(own, n) for n in range(1, NZ)])
    merged = swap(merge(z, message, rows), PLANE)
    mixed = mix(z, message)
    sums = [along_z(mixed[n], n) for n in range(1, NZ)]
    return back(atom_counts, out_grad, merged), total(mixed[0], sums)


def solution(mesh):
    split = Mesh(mesh.devices.reshape([size for _, size in AXES]), NAMES)
    placed = (
        P(NAMES, None, None),
        P(NAMES, None, None),
        P(NAMES, None),
        P(NAMES),
        P(None, NAMES, None),
    )
    return jax.shard_map(
        shards,
        mesh=split,
        in_specs=placed,
        out_specs=(P(NAMES, None, None), P(None, NAMES, None)),
        check_vma=False,
    )
```

```python
import jax
import jax.numpy as jnp
from jax import lax
from jax.experimental import pallas as pl
from jax.experimental.pallas import tpu as pltpu
from jax.sharding import Mesh, PartitionSpec as P

AXES = (("z", 8), ("xl", 2), ("core", 2), ("y", 4), ("xh", 2))
NAMES = tuple(name for name, _ in AXES)
PLANE = ("xl", "core", "y", "xh")
NZ = 8
NG = 32
ROWS = 2
PER = NZ * ROWS
D = 512
E = 16
K = 4
M = 256
STACK_MIB = 62
MERGE_MIB = 60
MIX_MIB = 24
BACK_MIB = 24
F32 = jnp.float32
BF16 = jnp.bfloat16
LANES = 128
TILES = D // LANES
PART = E * ROWS
WIDTH = NZ * PART
CARD = K * TILES
GROUP = 8
STEP = GROUP * K


def vmem(mib):
    return pltpu.CompilerParams(vmem_limit_bytes=mib * 1024 * 1024)


def row_of(shape, dim):
    return lax.broadcasted_iota(jnp.int32, shape, dim)


def order():
    to = row_of((D, 1), 0)
    source = (((to >> 1) & (NZ - 1)) << 6) + ((to >> 4) << 1) + (to & 1)
    return jnp.where(source == row_of((1, D), 1), 1.0, 0.0).astype(BF16)


def matmul(a, b, dims):
    return lax.dot_general(a, b, (dims, ((), ())), preferred_element_type=F32)


def masked_of(grad, count):
    return jnp.where(row_of((M, 1), 0) < count, grad, jnp.zeros_like(grad))


def card(fixed):
    lane = row_of((E, LANES), 1)
    row = row_of((E, LANES), 0)
    high = (fixed >> 6).astype(F32) * (1.0 / 64.0)
    low = (fixed & 63).astype(F32) * (1.0 / 4096.0)
    first = jnp.where(lane == row, 1.0, 0.0).astype(BF16)
    second = jnp.where(lane == row + E, 1.0, 0.0).astype(BF16)
    return matmul(high.astype(BF16), first, ((1,), (0,))) + matmul(low.astype(BF16), second, ((1,), (0,)))


def outer_kernel(counts, fixed, x, grad, out, xs, grads, pick, held, sheet, ins, outs):
    def fetch(k):
        return (
            pltpu.make_async_copy(x.at[k], xs.at[k], ins.at[2 * k]),
            pltpu.make_async_copy(grad.at[k], grads.at[k], ins.at[2 * k + 1]),
        )

    def send(k):
        place = pl.ds(k * TILES, TILES)
        return pltpu.make_async_copy(held.at[:, place], out.at[:, place], outs.at[k])

    send_card = pltpu.make_async_copy(held.at[:, pl.ds(CARD, 1)], out.at[:, pl.ds(CARD, 1)], outs.at[K])
    fetches = [fetch(k) for k in range(K)]
    for side in range(2):
        for pair in fetches:
            pair[side].start()
    sheet[...] = jnp.zeros_like(sheet)
    sheet[0:K] = card(fixed[...])
    held[:, CARD] = jnp.broadcast_to(sheet[...].astype(BF16)[None], (NG, PER, LANES))
    send_card.start()
    pick[...] = order()
    for k in range(K):
        fetches[k][0].wait()
    moved = matmul(xs[...].reshape(K * M, D), pick[...], ((1,), (1,))).astype(BF16)
    for k in range(K):
        turned = moved[k * M : (k + 1) * M].T
        fetches[k][1].wait()
        product = matmul(turned, masked_of(grads[k], counts[k]), ((1,), (0,))).astype(BF16)
        for tile in range(TILES):
            part = product[:, tile * LANES : (tile + 1) * LANES]
            held[:, k * TILES + tile] = part.reshape(NG, PER, LANES)
        send(k).start()
    send_card.wait()
    for k in range(K):
        send(k).wait()


ANY = pl.BlockSpec(memory_space=pl.ANY)
SCALARS = pl.BlockSpec(memory_space=pltpu.SMEM)
WHOLE = pl.BlockSpec(memory_space=pltpu.VMEM)


def outer(counts, fixed, x, grad):
    return pl.pallas_call(
        outer_kernel,
        in_specs=[SCALARS, WHOLE, ANY, ANY],
        out_specs=ANY,
        scratch_shapes=[
            pltpu.VMEM((K, M, D), BF16),
            pltpu.VMEM((K, M, D), BF16),
            pltpu.VMEM((D, D), BF16),
            pltpu.VMEM((NG, CARD + 1, PER, LANES), BF16),
            pltpu.VMEM((PER, LANES), F32),
            pltpu.SemaphoreType.DMA((2 * K,)),
            pltpu.SemaphoreType.DMA((K + 1,)),
        ],
        out_shape=jax.ShapeDtypeStruct((NG, CARD + 1, PER, LANES), BF16),
        compiler_params=vmem(56),
        cost_estimate=pl.CostEstimate(flops=2 * K * D * D * (M + M), bytes_accessed=4 << 20, transcendentals=0),
        name="outer",
    )(counts, fixed, x, grad)


def one_hot(found):
    return jnp.where(found, 1.0, 0.0).astype(BF16)


def line_of(part, z, away):
    line = (z + away * ((part & (WIDTH - 1)) >> 5) + NZ) & (NZ - 1)
    return (line << 1) + (part & 1)


def source_of(part):
    return ((part >> 1) & (E - 1)) + ((part >> 8) << 4)


HALF = 8
LINES = HALF // ROWS


def stack_kernel(z, *refs):
    *blocks, out = refs
    for n, block in enumerate(blocks):
        line = (z[0] - n + NZ) & (NZ - 1)
        half, place = line // LINES, (line & (LINES - 1)) * PART
        for part in range(2):
            out[half, pl.ds(pl.multiple_of(part * LINES * PART + place, PART), PART)] = block[...]


def stack(z, blocks):
    return pl.pallas_call(
        stack_kernel,
        in_specs=[SCALARS] + [WHOLE] * NZ,
        out_specs=WHOLE,
        out_shape=jax.ShapeDtypeStruct((2, WIDTH, D), BF16),
        compiler_params=vmem(STACK_MIB),
        cost_estimate=pl.CostEstimate(flops=0, bytes_accessed=6 * WIDTH * D, transcendentals=0),
        name="stack",
    )(z, *blocks)


GROUPS = NG // GROUP
TALL = STEP * PER


def merge_kernel(message, rows, out, cards, weights, wide, held, ins, outs):
    fetch_cards = pltpu.make_async_copy(message.at[:, pl.ds(CARD, 1)], cards, ins.at[0])
    fetch_rows = pltpu.make_async_copy(rows, weights, ins.at[1])

    def send(n):
        place = pl.ds(n * GROUP, GROUP)
        return pltpu.make_async_copy(held.at[place], out.at[place], outs.at[n])

    fetch_cards.start()
    fetch_rows.start()
    system = row_of((NG * K, 1), 0)
    pick = one_hot(((system >> 2) << 4) + (system & (K - 1)) == row_of((1, NG * PER), 1))
    col = row_of((1, WIDTH), 1)
    source = ((col >> 1) & (E - 1)) + ((col >> 7) << 4)
    widen = one_hot(row_of((LANES, 1), 0) == source)
    place = (((col >> 5) & (LINES - 1)) << 1) + (col & 1)
    same = row_of((HALF, 1), 0) == place
    fetch_cards.wait()
    values = matmul(pick, cards[...].reshape(NG * PER, LANES), ((1,), (0,))).astype(BF16)
    wide[...] = matmul(values, widen, ((1,), (0,)))
    fetch_rows.wait()
    for n in range(GROUPS):
        tall = jnp.where(same[None], wide[n * STEP : (n + 1) * STEP][:, None, :], 0.0)
        factor = tall.reshape(STEP * HALF, WIDTH).astype(BF16)
        halves = [matmul(factor, weights[h], ((1,), (0,))).reshape(STEP, HALF, D) for h in range(2)]
        merged = jnp.concatenate(halves, axis=1).astype(BF16)
        held[n * GROUP : (n + 1) * GROUP] = merged.reshape(GROUP, K, PER, D)
        send(n).start()
    for n in range(GROUPS):
        send(n).wait()


def merge(message, rows):
    return pl.pallas_call(
        merge_kernel,
        in_specs=[ANY, ANY],
        out_specs=ANY,
        scratch_shapes=[
            pltpu.VMEM((NG, 1, PER, LANES), BF16),
            pltpu.VMEM((2, WIDTH, D), BF16),
            pltpu.VMEM((NG * K, WIDTH), F32),
            pltpu.VMEM((NG, K, PER, D), BF16),
            pltpu.SemaphoreType.DMA((2,)),
            pltpu.SemaphoreType.DMA((GROUPS,)),
        ],
        out_shape=jax.ShapeDtypeStruct((NG, K, PER, D), BF16),
        compiler_params=vmem(MERGE_MIB),
        cost_estimate=pl.CostEstimate(flops=2 * NG * K * PER * WIDTH * D, bytes_accessed=3 << 20, transcendentals=0),
        name="merge",
    )(message, rows)


def mix_kernel(z, message, *refs):
    out, (held, total, low, ins, outs) = refs[:NZ], refs[NZ:]
    fetches = []
    for n in range(GROUPS):
        place = pl.ds(n * GROUP, GROUP)
        fetches.append(pltpu.make_async_copy(message.at[place], held.at[place], ins.at[n]))
        fetches[n].start()
    tall = row_of((1, TALL), 1)
    pick = one_hot(row_of((GROUP * PER, 1), 0) == (((tall >> 4) & (GROUP - 1)) << 4) + (tall >> 7))
    part = row_of((2 * WIDTH, 1), 0)
    widen = one_hot(source_of(part) == row_of((1, LANES), 1))
    same = line_of(part, z[0], 1) == (tall & (PER - 1))
    for n in range(GROUPS):
        fetches[n].wait()
        place = slice(n * GROUP, (n + 1) * GROUP)
        tiles = held[place, CARD].reshape(GROUP * PER, LANES)
        values = matmul(tiles, pick, ((0,), (0,))).astype(BF16)
        factor = jnp.where(same, matmul(widen, values, ((1,), (0,))), 0.0).astype(BF16)
        columns = []
        for tile in range(TILES):
            pieces = [held[place, k * TILES + tile].reshape(GROUP * PER, LANES) for k in range(K)]
            columns.append(jnp.concatenate(pieces, axis=0))
        both = matmul(factor, jnp.concatenate(columns, axis=1), ((1,), (0,)))
        sums = both[:WIDTH] + both[WIDTH:]
        total[...] = sums if n == 0 else total[...] + sums
    low[...] = total[...].astype(BF16)
    out[0][...] = total[:PART]
    sends = []
    for n in range(1, NZ):
        sends.append(pltpu.make_async_copy(low.at[pl.ds(n * PART, PART)], out[n], outs.at[n - 1]))
    for copy in sends:
        copy.start()
    for copy in sends:
        copy.wait()


def mix(z, message):
    return pl.pallas_call(
        mix_kernel,
        in_specs=[SCALARS, ANY],
        out_specs=[WHOLE] + [ANY] * (NZ - 1),
        scratch_shapes=[
            pltpu.VMEM((NG, CARD + 1, PER, LANES), BF16),
            pltpu.VMEM((WIDTH, D), F32),
            pltpu.VMEM((WIDTH, D), BF16),
            pltpu.SemaphoreType.DMA((GROUPS,)),
            pltpu.SemaphoreType.DMA((NZ - 1,)),
        ],
        out_shape=[jax.ShapeDtypeStruct((PART, D), F32)]
        + [jax.ShapeDtypeStruct((PART, D), BF16)] * (NZ - 1),
        compiler_params=vmem(MIX_MIB),
        cost_estimate=pl.CostEstimate(flops=4 * NG * K * PER * WIDTH * D, bytes_accessed=3 << 20, transcendentals=0),
        name="mix",
    )(z, message)


def total_kernel(own, *refs):
    *sums, out = refs
    total = own[...]
    for part in sums:
        total += part[...].astype(F32)
    for e in range(E):
        out[e] = total[ROWS * e : ROWS * (e + 1)]


def total(own, sums):
    return pl.pallas_call(
        total_kernel,
        out_shape=jax.ShapeDtypeStruct((E, ROWS, D), F32),
        compiler_params=vmem(8),
        cost_estimate=pl.CostEstimate(flops=WIDTH * D, bytes_accessed=5 * WIDTH * D, transcendentals=0),
        name="total",
    )(own, *sums)


def back_kernel(counts, grad, merged, out, pick, held, outs):
    def send(k):
        return pltpu.make_async_copy(held.at[k], out.at[k], outs.at[k])

    pick[...] = order()
    for k in range(K):
        masked = masked_of(grad[k], counts[k])
        moved = matmul(masked, merged[:, k].reshape(D, D), ((1,), (1,))).astype(BF16)
        held[k] = matmul(moved, pick[...], ((1,), (0,))).astype(BF16)
        send(k).start()
    for k in range(K):
        send(k).wait()


def back(counts, grad, merged):
    return pl.pallas_call(
        back_kernel,
        in_specs=[SCALARS, WHOLE, WHOLE],
        out_specs=ANY,
        scratch_shapes=[
            pltpu.VMEM((D, D), BF16),
            pltpu.VMEM((K, M, D), BF16),
            pltpu.SemaphoreType.DMA((K,)),
        ],
        out_shape=jax.ShapeDtypeStruct((K, M, D), BF16),
        compiler_params=vmem(BACK_MIB),
        cost_estimate=pl.CostEstimate(flops=4 * K * M * D * D, bytes_accessed=4 << 20, transcendentals=0),
        name="back",
    )(counts, grad, merged)


def swap(array, axes):
    return lax.all_to_all(array, axes, 0, 0, tiled=True)


def along_z(array, by):
    return lax.ppermute(array, "z", [(i, (i + by) % NZ) for i in range(NZ)])


def shards(inputs, out_grad, coeff_fixed, atom_counts, experts):
    z = lax.axis_index("z").astype(jnp.int32).reshape(1)
    message = swap(outer(atom_counts, coeff_fixed, inputs, out_grad), PLANE)
    own = experts.reshape(PART, D)
    rows = stack(z, [own] + [along_z(own, n) for n in range(1, NZ)])
    merged = swap(merge(message, rows), PLANE)
    mixed = mix(z, message)
    sums = [along_z(mixed[n], n) for n in range(1, NZ)]
    return back(atom_counts, out_grad, merged), total(mixed[0], sums)


def solution(mesh):
    split = Mesh(mesh.devices.reshape([size for _, size in AXES]), NAMES)
    placed = (
        P(NAMES, None, None),
        P(NAMES, None, None),
        P(NAMES, None),
        P(NAMES),
        P(None, NAMES, None),
    )
    return jax.shard_map(
        shards,
        mesh=split,
        in_specs=placed,
        out_specs=(P(NAMES, None, None), P(None, NAMES, None)),
        check_vma=False,
    )
```

```python
import jax
import jax.numpy as jnp
from jax import lax
from jax.experimental import pallas as pl
from jax.experimental.pallas import tpu as pltpu
from jax.sharding import Mesh, PartitionSpec as P

AXES = (("z", 8), ("xl", 2), ("core", 2), ("y", 4), ("xh", 2))
NAMES = tuple(name for name, _ in AXES)
PLANE = ("xl", "core", "y", "xh")
NZ = 8
NG = 32
ROWS = 2
PER = NZ * ROWS
D = 512
E = 16
K = 4
M = 256
STACK_MIB = 62
MERGE_MIB = 60
MIX_MIB = 24
BACK_MIB = 24
F32 = jnp.float32
BF16 = jnp.bfloat16
LANES = 128
TILES = D // LANES
PART = E * ROWS
WIDTH = NZ * PART
CARD = K * TILES
GROUP = 8
STEP = GROUP * K


def vmem(mib):
    return pltpu.CompilerParams(vmem_limit_bytes=mib * 1024 * 1024)


def row_of(shape, dim):
    return lax.broadcasted_iota(jnp.int32, shape, dim)


def order():
    to = row_of((D, 1), 0)
    source = (((to >> 1) & (NZ - 1)) << 6) + ((to >> 4) << 1) + (to & 1)
    return jnp.where(source == row_of((1, D), 1), 1.0, 0.0).astype(BF16)


def matmul(a, b, dims):
    return lax.dot_general(a, b, (dims, ((), ())), preferred_element_type=F32)


def masked_of(grad, count):
    return jnp.where(row_of((M, 1), 0) < count, grad, jnp.zeros_like(grad))


def card(fixed):
    lane = row_of((E, LANES), 1)
    row = row_of((E, LANES), 0)
    high = (fixed >> 6).astype(F32) * (1.0 / 64.0)
    low = (fixed & 63).astype(F32) * (1.0 / 4096.0)
    first = jnp.where(lane == row, 1.0, 0.0).astype(BF16)
    second = jnp.where(lane == row + E, 1.0, 0.0).astype(BF16)
    return matmul(high.astype(BF16), first, ((1,), (0,))) + matmul(low.astype(BF16), second, ((1,), (0,)))


def outer_kernel(counts, fixed, x, grad, out, xs, grads, pick, held, sheet, ins, outs):
    def fetch(k):
        return (
            pltpu.make_async_copy(x.at[k], xs.at[k], ins.at[2 * k]),
            pltpu.make_async_copy(grad.at[k], grads.at[k], ins.at[2 * k + 1]),
        )

    def send(k):
        place = pl.ds(k * TILES, TILES)
        return pltpu.make_async_copy(held.at[:, place], out.at[:, place], outs.at[k])

    send_card = pltpu.make_async_copy(held.at[:, pl.ds(CARD, 1)], out.at[:, pl.ds(CARD, 1)], outs.at[K])
    fetches = [fetch(k) for k in range(K)]
    for side in range(2):
        for pair in fetches:
            pair[side].start()
    sheet[...] = jnp.zeros_like(sheet)
    sheet[0:K] = card(fixed[...])
    held[:, CARD] = jnp.broadcast_to(sheet[...].astype(BF16)[None], (NG, PER, LANES))
    send_card.start()
    pick[...] = order()
    for k in range(K):
        fetches[k][0].wait()
    moved = matmul(xs[...].reshape(K * M, D), pick[...], ((1,), (1,))).astype(BF16)
    for k in range(K):
        turned = moved[k * M : (k + 1) * M].T
        fetches[k][1].wait()
        product = matmul(turned, masked_of(grads[k], counts[k]), ((1,), (0,))).astype(BF16)
        for tile in range(TILES):
            part = product[:, tile * LANES : (tile + 1) * LANES]
            held[:, k * TILES + tile] = part.reshape(NG, PER, LANES)
        send(k).start()
    send_card.wait()
    for k in range(K):
        send(k).wait()


ANY = pl.BlockSpec(memory_space=pl.ANY)
SCALARS = pl.BlockSpec(memory_space=pltpu.SMEM)
WHOLE = pl.BlockSpec(memory_space=pltpu.VMEM)


def outer(counts, fixed, x, grad):
    return pl.pallas_call(
        outer_kernel,
        in_specs=[SCALARS, WHOLE, ANY, ANY],
        out_specs=ANY,
        scratch_shapes=[
            pltpu.VMEM((K, M, D), BF16),
            pltpu.VMEM((K, M, D), BF16),
            pltpu.VMEM((D, D), BF16),
            pltpu.VMEM((NG, CARD + 1, PER, LANES), BF16),
            pltpu.VMEM((PER, LANES), F32),
            pltpu.SemaphoreType.DMA((2 * K,)),
            pltpu.SemaphoreType.DMA((K + 1,)),
        ],
        out_shape=jax.ShapeDtypeStruct((NG, CARD + 1, PER, LANES), BF16),
        compiler_params=vmem(56),
        cost_estimate=pl.CostEstimate(flops=2 * K * D * D * (M + M), bytes_accessed=4 << 20, transcendentals=0),
        name="outer",
    )(counts, fixed, x, grad)


def one_hot(found):
    return jnp.where(found, 1.0, 0.0).astype(BF16)


def line_of(part, z, away):
    line = (z + away * ((part & (WIDTH - 1)) >> 5) + NZ) & (NZ - 1)
    return (line << 1) + (part & 1)


def source_of(part):
    return ((part >> 1) & (E - 1)) + ((part >> 8) << 4)


HALF = 8
LINES = HALF // ROWS
BACK = (0, 4, 2, 6, 1, 5, 3, 7)


def stack_kernel(z, near, far, out):
    for n in range(NZ):
        source = near if n < NZ // 2 else far
        block = source[(n % (NZ // 2)) * PART : (n % (NZ // 2) + 1) * PART]
        line = (z[0] - BACK[n] + NZ) & (NZ - 1)
        half, place = line // LINES, (line & (LINES - 1)) * PART
        for part in range(2):
            out[half, pl.ds(pl.multiple_of(part * LINES * PART + place, PART), PART)] = block


def stack(z, near, far):
    return pl.pallas_call(
        stack_kernel,
        in_specs=[SCALARS, WHOLE, WHOLE],
        out_specs=WHOLE,
        out_shape=jax.ShapeDtypeStruct((2, WIDTH, D), BF16),
        compiler_params=vmem(STACK_MIB),
        cost_estimate=pl.CostEstimate(flops=0, bytes_accessed=6 * WIDTH * D, transcendentals=0),
        name="stack",
    )(z, near, far)


GROUPS = NG // GROUP
TALL = STEP * PER


def merge_kernel(message, rows, out, cards, weights, wide, held, ins, outs):
    fetch_cards = pltpu.make_async_copy(message.at[:, pl.ds(CARD, 1)], cards, ins.at[0])
    fetch_rows = pltpu.make_async_copy(rows, weights, ins.at[1])

    def send(n):
        place = pl.ds(n * GROUP, GROUP)
        return pltpu.make_async_copy(held.at[place], out.at[place], outs.at[n])

    fetch_cards.start()
    fetch_rows.start()
    system = row_of((NG * K, 1), 0)
    pick = one_hot(((system >> 2) << 4) + (system & (K - 1)) == row_of((1, NG * PER), 1))
    col = row_of((1, WIDTH), 1)
    source = ((col >> 1) & (E - 1)) + ((col >> 7) << 4)
    widen = one_hot(row_of((LANES, 1), 0) == source)
    place = (((col >> 5) & (LINES - 1)) << 1) + (col & 1)
    same = row_of((HALF, 1), 0) == place
    fetch_cards.wait()
    values = matmul(pick, cards[...].reshape(NG * PER, LANES), ((1,), (0,))).astype(BF16)
    wide[...] = matmul(values, widen, ((1,), (0,)))
    fetch_rows.wait()
    for n in range(GROUPS):
        tall = jnp.where(same[None], wide[n * STEP : (n + 1) * STEP][:, None, :], 0.0)
        factor = tall.reshape(STEP * HALF, WIDTH).astype(BF16)
        halves = [matmul(factor, weights[h], ((1,), (0,))).reshape(STEP, HALF, D) for h in range(2)]
        merged = jnp.concatenate(halves, axis=1).astype(BF16)
        held[n * GROUP : (n + 1) * GROUP] = merged.reshape(GROUP, K, PER, D)
        send(n).start()
    for n in range(GROUPS):
        send(n).wait()


def merge(message, rows):
    return pl.pallas_call(
        merge_kernel,
        in_specs=[ANY, ANY],
        out_specs=ANY,
        scratch_shapes=[
            pltpu.VMEM((NG, 1, PER, LANES), BF16),
            pltpu.VMEM((2, WIDTH, D), BF16),
            pltpu.VMEM((NG * K, WIDTH), F32),
            pltpu.VMEM((NG, K, PER, D), BF16),
            pltpu.SemaphoreType.DMA((2,)),
            pltpu.SemaphoreType.DMA((GROUPS,)),
        ],
        out_shape=jax.ShapeDtypeStruct((NG, K, PER, D), BF16),
        compiler_params=vmem(MERGE_MIB),
        cost_estimate=pl.CostEstimate(flops=2 * NG * K * PER * WIDTH * D, bytes_accessed=3 << 20, transcendentals=0),
        name="merge",
    )(message, rows)


def mix_kernel(z, message, *refs):
    out, (held, total, low, ins, outs) = refs[:NZ], refs[NZ:]
    fetches = []
    for n in range(GROUPS):
        place = pl.ds(n * GROUP, GROUP)
        fetches.append(pltpu.make_async_copy(message.at[place], held.at[place], ins.at[n]))
        fetches[n].start()
    tall = row_of((1, TALL), 1)
    pick = one_hot(row_of((GROUP * PER, 1), 0) == (((tall >> 4) & (GROUP - 1)) << 4) + (tall >> 7))
    part = row_of((2 * WIDTH, 1), 0)
    widen = one_hot(source_of(part) == row_of((1, LANES), 1))
    same = line_of(part, z[0], 1) == (tall & (PER - 1))
    for n in range(GROUPS):
        fetches[n].wait()
        place = slice(n * GROUP, (n + 1) * GROUP)
        tiles = held[place, CARD].reshape(GROUP * PER, LANES)
        values = matmul(tiles, pick, ((0,), (0,))).astype(BF16)
        factor = jnp.where(same, matmul(widen, values, ((1,), (0,))), 0.0).astype(BF16)
        columns = []
        for tile in range(TILES):
            pieces = [held[place, k * TILES + tile].reshape(GROUP * PER, LANES) for k in range(K)]
            columns.append(jnp.concatenate(pieces, axis=0))
        both = matmul(factor, jnp.concatenate(columns, axis=1), ((1,), (0,)))
        sums = both[:WIDTH] + both[WIDTH:]
        total[...] = sums if n == 0 else total[...] + sums
    low[...] = total[...].astype(BF16)
    out[0][...] = total[:PART]
    sends = []
    for n in range(1, NZ):
        sends.append(pltpu.make_async_copy(low.at[pl.ds(n * PART, PART)], out[n], outs.at[n - 1]))
    for copy in sends:
        copy.start()
    for copy in sends:
        copy.wait()


def mix(z, message):
    return pl.pallas_call(
        mix_kernel,
        in_specs=[SCALARS, ANY],
        out_specs=[WHOLE] + [ANY] * (NZ - 1),
        scratch_shapes=[
            pltpu.VMEM((NG, CARD + 1, PER, LANES), BF16),
            pltpu.VMEM((WIDTH, D), F32),
            pltpu.VMEM((WIDTH, D), BF16),
            pltpu.SemaphoreType.DMA((GROUPS,)),
            pltpu.SemaphoreType.DMA((NZ - 1,)),
        ],
        out_shape=[jax.ShapeDtypeStruct((PART, D), F32)]
        + [jax.ShapeDtypeStruct((PART, D), BF16)] * (NZ - 1),
        compiler_params=vmem(MIX_MIB),
        cost_estimate=pl.CostEstimate(flops=4 * NG * K * PER * WIDTH * D, bytes_accessed=3 << 20, transcendentals=0),
        name="mix",
    )(z, message)


def total_kernel(own, *refs):
    *sums, out = refs
    total = own[...]
    for part in sums:
        total += part[...].astype(F32)
    for e in range(E):
        out[e] = total[ROWS * e : ROWS * (e + 1)]


def total(own, sums):
    return pl.pallas_call(
        total_kernel,
        out_shape=jax.ShapeDtypeStruct((E, ROWS, D), F32),
        compiler_params=vmem(8),
        cost_estimate=pl.CostEstimate(flops=WIDTH * D, bytes_accessed=5 * WIDTH * D, transcendentals=0),
        name="total",
    )(own, *sums)


def back_kernel(counts, grad, merged, out, pick, near, held, outs):
    def send(k):
        return pltpu.make_async_copy(held.at[k], out.at[k], outs.at[k])

    for k in range(K):
        masked = masked_of(grad[k], counts[k])
        near[k] = matmul(masked, merged[:, k].reshape(D, D), ((1,), (1,))).astype(BF16)
        if k == 0:
            pick[...] = order()
        if k % 2 == 1:
            done = matmul(near[k - 1 : k + 1].reshape(2 * M, D), pick[...], ((1,), (0,))).astype(BF16)
            held[k - 1 : k + 1] = done.reshape(2, M, D)
            send(k - 1).start()
            send(k).start()
    for k in range(K):
        send(k).wait()


def back(counts, grad, merged):
    return pl.pallas_call(
        back_kernel,
        in_specs=[SCALARS, WHOLE, WHOLE],
        out_specs=ANY,
        scratch_shapes=[
            pltpu.VMEM((D, D), BF16),
            pltpu.VMEM((K, M, D), BF16),
            pltpu.VMEM((K, M, D), BF16),
            pltpu.SemaphoreType.DMA((K,)),
        ],
        out_shape=jax.ShapeDtypeStruct((K, M, D), BF16),
        compiler_params=vmem(BACK_MIB),
        cost_estimate=pl.CostEstimate(flops=4 * K * M * D * D, bytes_accessed=4 << 20, transcendentals=0),
        name="back",
    )(counts, grad, merged)


def swap(array, axes):
    return lax.all_to_all(array, axes, 0, 0, tiled=True)


def along_z(array, by):
    return lax.ppermute(array, "z", [(i, (i + by) % NZ) for i in range(NZ)])


def shards(inputs, out_grad, coeff_fixed, atom_counts, experts):
    z = lax.axis_index("z").astype(jnp.int32).reshape(1)
    message = swap(outer(atom_counts, coeff_fixed, inputs, out_grad), PLANE)
    own = experts.reshape(PART, D)
    near = jnp.concatenate([own, along_z(own, 4)])
    near = jnp.concatenate([near, along_z(near, 2)])
    rows = stack(z, near, along_z(near, 1))
    merged = swap(merge(message, rows), PLANE)
    mixed = mix(z, message)
    sums = [along_z(mixed[n], n) for n in range(1, NZ)]
    return back(atom_counts, out_grad, merged), total(mixed[0], sums)


def solution(mesh):
    split = Mesh(mesh.devices.reshape([size for _, size in AXES]), NAMES)
    placed = (
        P(NAMES, None, None),
        P(NAMES, None, None),
        P(NAMES, None),
        P(NAMES),
        P(None, NAMES, None),
    )
    return jax.shard_map(
        shards,
        mesh=split,
        in_specs=placed,
        out_specs=(P(NAMES, None, None), P(None, NAMES, None)),
        check_vma=False,
    )
```

```python
import jax
import jax.numpy as jnp
from jax import lax
from jax.experimental import pallas as pl
from jax.experimental.pallas import tpu as pltpu
from jax.sharding import Mesh, PartitionSpec as P

AXES = (("z", 8), ("xl", 2), ("core", 2), ("y", 4), ("xh", 2))
NAMES = tuple(name for name, _ in AXES)
PLANE = ("xl", "core", "y", "xh")
NZ = 8
NG = 32
ROWS = 2
PER = NZ * ROWS
D = 512
E = 16
K = 4
M = 256
STACK_MIB = 62
MERGE_MIB = 60
MIX_MIB = 24
BACK_MIB = 24
F32 = jnp.float32
BF16 = jnp.bfloat16
LANES = 128
TILES = D // LANES
PART = E * ROWS
WIDTH = NZ * PART
CARD = K * TILES
GROUP = 8
STEP = GROUP * K


def vmem(mib):
    return pltpu.CompilerParams(vmem_limit_bytes=mib * 1024 * 1024)


def row_of(shape, dim):
    return lax.broadcasted_iota(jnp.int32, shape, dim)


def order():
    to = row_of((D, 1), 0)
    source = (((to >> 1) & (NZ - 1)) << 6) + ((to >> 4) << 1) + (to & 1)
    return jnp.where(source == row_of((1, D), 1), 1.0, 0.0).astype(BF16)


def matmul(a, b, dims):
    return lax.dot_general(a, b, (dims, ((), ())), preferred_element_type=F32)


def masked_of(grad, count):
    return jnp.where(row_of((M, 1), 0) < count, grad, jnp.zeros_like(grad))


def card(fixed):
    lane = row_of((E, LANES), 1)
    row = row_of((E, LANES), 0)
    high = (fixed >> 6).astype(F32) * (1.0 / 64.0)
    low = (fixed & 63).astype(F32) * (1.0 / 4096.0)
    first = jnp.where(lane == row, 1.0, 0.0).astype(BF16)
    second = jnp.where(lane == row + E, 1.0, 0.0).astype(BF16)
    return matmul(high.astype(BF16), first, ((1,), (0,))) + matmul(low.astype(BF16), second, ((1,), (0,)))


def outer_kernel(counts, fixed, x, grad, out, xs, grads, pick, held, sheet, ins, outs):
    def fetch(k):
        return (
            pltpu.make_async_copy(x.at[k], xs.at[k], ins.at[2 * k]),
            pltpu.make_async_copy(grad.at[k], grads.at[k], ins.at[2 * k + 1]),
        )

    def send(k):
        place = pl.ds(k * TILES, TILES)
        return pltpu.make_async_copy(held.at[:, place], out.at[:, place], outs.at[k])

    send_card = pltpu.make_async_copy(held.at[:, pl.ds(CARD, 1)], out.at[:, pl.ds(CARD, 1)], outs.at[K])
    fetches = [fetch(k) for k in range(K)]
    for side in range(2):
        for pair in fetches:
            pair[side].start()
    sheet[...] = jnp.zeros_like(sheet)
    sheet[0:K] = card(fixed[...])
    held[:, CARD] = jnp.broadcast_to(sheet[...].astype(BF16)[None], (NG, PER, LANES))
    send_card.start()
    pick[...] = order()
    for k in range(K):
        fetches[k][0].wait()
    moved = matmul(xs[...].reshape(K * M, D), pick[...], ((1,), (1,))).astype(BF16)
    for k in range(K):
        turned = moved[k * M : (k + 1) * M].T
        fetches[k][1].wait()
        product = matmul(turned, masked_of(grads[k], counts[k]), ((1,), (0,))).astype(BF16)
        for tile in range(TILES):
            part = product[:, tile * LANES : (tile + 1) * LANES]
            held[:, k * TILES + tile] = part.reshape(NG, PER, LANES)
        send(k).start()
    send_card.wait()
    for k in range(K):
        send(k).wait()


ANY = pl.BlockSpec(memory_space=pl.ANY)
SCALARS = pl.BlockSpec(memory_space=pltpu.SMEM)
WHOLE = pl.BlockSpec(memory_space=pltpu.VMEM)


def outer(counts, fixed, x, grad):
    return pl.pallas_call(
        outer_kernel,
        in_specs=[SCALARS, WHOLE, ANY, ANY],
        out_specs=ANY,
        scratch_shapes=[
            pltpu.VMEM((K, M, D), BF16),
            pltpu.VMEM((K, M, D), BF16),
            pltpu.VMEM((D, D), BF16),
            pltpu.VMEM((NG, CARD + 1, PER, LANES), BF16),
            pltpu.VMEM((PER, LANES), F32),
            pltpu.SemaphoreType.DMA((2 * K,)),
            pltpu.SemaphoreType.DMA((K + 1,)),
        ],
        out_shape=jax.ShapeDtypeStruct((NG, CARD + 1, PER, LANES), BF16),
        compiler_params=vmem(56),
        cost_estimate=pl.CostEstimate(flops=2 * K * D * D * (M + M), bytes_accessed=4 << 20, transcendentals=0),
        name="outer",
    )(counts, fixed, x, grad)


def one_hot(found):
    return jnp.where(found, 1.0, 0.0).astype(BF16)


def line_of(part, z, away):
    line = (z + away * ((part & (WIDTH - 1)) >> 5) + NZ) & (NZ - 1)
    return (line << 1) + (part & 1)


def source_of(part):
    return ((part >> 1) & (E - 1)) + ((part >> 8) << 4)


HALF = 8
LINES = HALF // ROWS
BACK = (0, 4, 2, 6, 1, 5, 3, 7)


def stack_kernel(z, near, far, out):
    for n in range(NZ):
        source = near if n < NZ // 2 else far
        block = source[(n % (NZ // 2)) * PART : (n % (NZ // 2) + 1) * PART]
        line = (z[0] - BACK[n] + NZ) & (NZ - 1)
        half, place = line // LINES, (line & (LINES - 1)) * PART
        for part in range(2):
            out[half, pl.ds(pl.multiple_of(part * LINES * PART + place, PART), PART)] = block


def stack(z, near, far):
    return pl.pallas_call(
        stack_kernel,
        in_specs=[SCALARS, WHOLE, WHOLE],
        out_specs=WHOLE,
        out_shape=jax.ShapeDtypeStruct((2, WIDTH, D), BF16),
        compiler_params=vmem(STACK_MIB),
        cost_estimate=pl.CostEstimate(flops=0, bytes_accessed=6 * WIDTH * D, transcendentals=0),
        name="stack",
    )(z, near, far)


GROUPS = NG // GROUP
TALL = STEP * PER


def merge_kernel(message, rows, out, cards, weights, wide, held, ins, outs):
    fetch_cards = pltpu.make_async_copy(message.at[:, pl.ds(CARD, 1)], cards, ins.at[0])
    fetch_rows = pltpu.make_async_copy(rows, weights, ins.at[1])

    def send(n):
        place = pl.ds(n * GROUP, GROUP)
        return pltpu.make_async_copy(held.at[place], out.at[place], outs.at[n])

    fetch_cards.start()
    fetch_rows.start()
    system = row_of((NG * K, 1), 0)
    pick = one_hot(((system >> 2) << 4) + (system & (K - 1)) == row_of((1, NG * PER), 1))
    col = row_of((1, WIDTH), 1)
    source = ((col >> 1) & (E - 1)) + ((col >> 7) << 4)
    widen = one_hot(row_of((LANES, 1), 0) == source)
    place = (((col >> 5) & (LINES - 1)) << 1) + (col & 1)
    same = row_of((HALF, 1), 0) == place
    fetch_cards.wait()
    values = matmul(pick, cards[...].reshape(NG * PER, LANES), ((1,), (0,))).astype(BF16)
    wide[...] = matmul(values, widen, ((1,), (0,)))
    fetch_rows.wait()
    for n in range(GROUPS):
        tall = jnp.where(same[None], wide[n * STEP : (n + 1) * STEP][:, None, :], 0.0)
        factor = tall.reshape(STEP * HALF, WIDTH).astype(BF16)
        halves = [matmul(factor, weights[h], ((1,), (0,))).reshape(STEP, HALF, D) for h in range(2)]
        merged = jnp.concatenate(halves, axis=1).astype(BF16)
        held[n * GROUP : (n + 1) * GROUP] = merged.reshape(GROUP, K, PER, D)
        send(n).start()
    for n in range(GROUPS):
        send(n).wait()


def merge(message, rows):
    return pl.pallas_call(
        merge_kernel,
        in_specs=[ANY, ANY],
        out_specs=ANY,
        scratch_shapes=[
            pltpu.VMEM((NG, 1, PER, LANES), BF16),
            pltpu.VMEM((2, WIDTH, D), BF16),
            pltpu.VMEM((NG * K, WIDTH), F32),
            pltpu.VMEM((NG, K, PER, D), BF16),
            pltpu.SemaphoreType.DMA((2,)),
            pltpu.SemaphoreType.DMA((GROUPS,)),
        ],
        out_shape=jax.ShapeDtypeStruct((NG, K, PER, D), BF16),
        compiler_params=vmem(MERGE_MIB),
        cost_estimate=pl.CostEstimate(flops=2 * NG * K * PER * WIDTH * D, bytes_accessed=3 << 20, transcendentals=0),
        name="merge",
    )(message, rows)


def mix_kernel(z, message, *refs):
    out, (held, total, low, ins, outs) = refs[:NZ], refs[NZ:]
    fetches = []
    for n in range(GROUPS):
        place = pl.ds(n * GROUP, GROUP)
        fetches.append(pltpu.make_async_copy(message.at[place], held.at[place], ins.at[n]))
        fetches[n].start()
    tall = row_of((1, TALL), 1)
    pick = one_hot(row_of((GROUP * PER, 1), 0) == (((tall >> 4) & (GROUP - 1)) << 4) + (tall >> 7))
    part = row_of((2 * WIDTH, 1), 0)
    widen = one_hot(source_of(part) == row_of((1, LANES), 1))
    same = line_of(part, z[0], 1) == (tall & (PER - 1))
    for n in range(GROUPS):
        fetches[n].wait()
        place = slice(n * GROUP, (n + 1) * GROUP)
        tiles = held[place, CARD].reshape(GROUP * PER, LANES)
        values = matmul(tiles, pick, ((0,), (0,))).astype(BF16)
        factor = jnp.where(same, matmul(widen, values, ((1,), (0,))), 0.0).astype(BF16)
        columns = []
        for tile in range(TILES):
            pieces = [held[place, k * TILES + tile].reshape(GROUP * PER, LANES) for k in range(K)]
            columns.append(jnp.concatenate(pieces, axis=0))
        both = matmul(factor, jnp.concatenate(columns, axis=1), ((1,), (0,)))
        sums = both[:WIDTH] + both[WIDTH:]
        total[...] = sums if n == 0 else total[...] + sums
    low[...] = total[...].astype(BF16)
    out[0][...] = total[:PART]
    sends = []
    for n in range(1, NZ):
        sends.append(pltpu.make_async_copy(low.at[pl.ds(n * PART, PART)], out[n], outs.at[n - 1]))
    for copy in sends:
        copy.start()
    for copy in sends:
        copy.wait()


def mix(z, message):
    return pl.pallas_call(
        mix_kernel,
        in_specs=[SCALARS, ANY],
        out_specs=[WHOLE] + [ANY] * (NZ - 1),
        scratch_shapes=[
            pltpu.VMEM((NG, CARD + 1, PER, LANES), BF16),
            pltpu.VMEM((WIDTH, D), F32),
            pltpu.VMEM((WIDTH, D), BF16),
            pltpu.SemaphoreType.DMA((GROUPS,)),
            pltpu.SemaphoreType.DMA((NZ - 1,)),
        ],
        out_shape=[jax.ShapeDtypeStruct((PART, D), F32)]
        + [jax.ShapeDtypeStruct((PART, D), BF16)] * (NZ - 1),
        compiler_params=vmem(MIX_MIB),
        cost_estimate=pl.CostEstimate(flops=4 * NG * K * PER * WIDTH * D, bytes_accessed=3 << 20, transcendentals=0),
        name="mix",
    )(z, message)


def total_kernel(own, *refs):
    *sums, out = refs
    total = own[...]
    for part in sums:
        total += part[...].astype(F32)
    for e in range(E):
        out[e] = total[ROWS * e : ROWS * (e + 1)]


def total(own, sums):
    return pl.pallas_call(
        total_kernel,
        out_shape=jax.ShapeDtypeStruct((E, ROWS, D), F32),
        compiler_params=vmem(8),
        cost_estimate=pl.CostEstimate(flops=WIDTH * D, bytes_accessed=5 * WIDTH * D, transcendentals=0),
        name="total",
    )(own, *sums)


def back_kernel(counts, grad, merged, out, pick, near, held, outs):
    def send(k):
        return pltpu.make_async_copy(held.at[k], out.at[k], outs.at[k])

    pick[...] = order()
    for k in range(K):
        masked = masked_of(grad[k], counts[k])
        near[k] = matmul(masked, merged[:, k].reshape(D, D), ((1,), (1,))).astype(BF16)
        if k == 1 or k == 3:
            for system in (k - 1, k):
                held[system] = matmul(near[system], pick[...], ((1,), (0,))).astype(BF16)
                send(system).start()
    for k in range(K):
        send(k).wait()


def back(counts, grad, merged):
    return pl.pallas_call(
        back_kernel,
        in_specs=[SCALARS, WHOLE, WHOLE],
        out_specs=ANY,
        scratch_shapes=[
            pltpu.VMEM((D, D), BF16),
            pltpu.VMEM((K, M, D), BF16),
            pltpu.VMEM((K, M, D), BF16),
            pltpu.SemaphoreType.DMA((K,)),
        ],
        out_shape=jax.ShapeDtypeStruct((K, M, D), BF16),
        compiler_params=vmem(BACK_MIB),
        cost_estimate=pl.CostEstimate(flops=4 * K * M * D * D, bytes_accessed=4 << 20, transcendentals=0),
        name="back",
    )(counts, grad, merged)


def swap(array, axes):
    return lax.all_to_all(array, axes, 0, 0, tiled=True)


def along_z(array, by):
    return lax.ppermute(array, "z", [(i, (i + by) % NZ) for i in range(NZ)])


def shards(inputs, out_grad, coeff_fixed, atom_counts, experts):
    z = lax.axis_index("z").astype(jnp.int32).reshape(1)
    message = swap(outer(atom_counts, coeff_fixed, inputs, out_grad), PLANE)
    own = experts.reshape(PART, D)
    near = jnp.concatenate([own, along_z(own, 4)])
    near = jnp.concatenate([near, along_z(near, 2)])
    rows = stack(z, near, along_z(near, 1))
    merged = swap(merge(message, rows), PLANE)
    mixed = mix(z, message)
    sums = [along_z(mixed[n], n) for n in range(1, NZ)]
    return back(atom_counts, out_grad, merged), total(mixed[0], sums)


def solution(mesh):
    split = Mesh(mesh.devices.reshape([size for _, size in AXES]), NAMES)
    placed = (
        P(NAMES, None, None),
        P(NAMES, None, None),
        P(NAMES, None),
        P(NAMES),
        P(None, NAMES, None),
    )
    return jax.shard_map(
        shards,
        mesh=split,
        in_specs=placed,
        out_specs=(P(NAMES, None, None), P(None, NAMES, None)),
        check_vma=False,
    )
```

```python
import jax
import jax.numpy as jnp
from jax import lax
from jax.experimental import pallas as pl
from jax.experimental.pallas import tpu as pltpu
from jax.sharding import Mesh, PartitionSpec as P

AXES = (("z", 8), ("xl", 2), ("core", 2), ("y", 4), ("xh", 2))
NAMES = tuple(name for name, _ in AXES)
PLANE = ("xl", "core", "y", "xh")
NZ = 8
NG = 32
ROWS = 2
PER = NZ * ROWS
D = 512
E = 16
K = 4
M = 256
STACK_MIB = 62
MERGE_MIB = 60
MIX_MIB = 24
BACK_MIB = 24
F32 = jnp.float32
BF16 = jnp.bfloat16
LANES = 128
TILES = D // LANES
PART = E * ROWS
WIDTH = NZ * PART
CARD = K * TILES
GROUP = 8
STEP = GROUP * K


def vmem(mib):
    return pltpu.CompilerParams(vmem_limit_bytes=mib * 1024 * 1024)


def row_of(shape, dim):
    return lax.broadcasted_iota(jnp.int32, shape, dim)


def order():
    to = row_of((D, 1), 0)
    source = (((to >> 1) & (NZ - 1)) << 6) + ((to >> 4) << 1) + (to & 1)
    return jnp.where(source == row_of((1, D), 1), 1.0, 0.0).astype(BF16)


def matmul(a, b, dims):
    return lax.dot_general(a, b, (dims, ((), ())), preferred_element_type=F32)


def masked_of(grad, count):
    return jnp.where(row_of((M, 1), 0) < count, grad, jnp.zeros_like(grad))


def card(fixed):
    lane = row_of((E, LANES), 1)
    row = row_of((E, LANES), 0)
    high = (fixed >> 6).astype(F32) * (1.0 / 64.0)
    low = (fixed & 63).astype(F32) * (1.0 / 4096.0)
    first = jnp.where(lane == row, 1.0, 0.0).astype(BF16)
    second = jnp.where(lane == row + E, 1.0, 0.0).astype(BF16)
    return matmul(high.astype(BF16), first, ((1,), (0,))) + matmul(low.astype(BF16), second, ((1,), (0,)))


def outer_kernel(counts, fixed, x, grad, out, xs, grads, pick, held, sheet, ins, outs):
    def fetch(k):
        return (
            pltpu.make_async_copy(x.at[k], xs.at[k], ins.at[2 * k]),
            pltpu.make_async_copy(grad.at[k], grads.at[k], ins.at[2 * k + 1]),
        )

    def send(k):
        place = pl.ds(k * TILES, TILES)
        return pltpu.make_async_copy(held.at[:, place], out.at[:, place], outs.at[k])

    send_card = pltpu.make_async_copy(held.at[:, pl.ds(CARD, 1)], out.at[:, pl.ds(CARD, 1)], outs.at[K])
    fetches = [fetch(k) for k in range(K)]
    for side in range(2):
        for pair in fetches:
            pair[side].start()
    sheet[...] = jnp.zeros_like(sheet)
    sheet[0:K] = card(fixed[...])
    held[:, CARD] = jnp.broadcast_to(sheet[...].astype(BF16)[None], (NG, PER, LANES))
    send_card.start()
    pick[...] = order()
    for k in range(K):
        fetches[k][0].wait()
    moved = matmul(xs[...].reshape(K * M, D), pick[...], ((1,), (1,))).astype(BF16)
    for k in range(K):
        turned = moved[k * M : (k + 1) * M].T
        fetches[k][1].wait()
        product = matmul(turned, masked_of(grads[k], counts[k]), ((1,), (0,))).astype(BF16)
        for tile in range(TILES):
            part = product[:, tile * LANES : (tile + 1) * LANES]
            held[:, k * TILES + tile] = part.reshape(NG, PER, LANES)
        send(k).start()
    send_card.wait()
    for k in range(K):
        send(k).wait()


ANY = pl.BlockSpec(memory_space=pl.ANY)
SCALARS = pl.BlockSpec(memory_space=pltpu.SMEM)
WHOLE = pl.BlockSpec(memory_space=pltpu.VMEM)


def outer(counts, fixed, x, grad):
    return pl.pallas_call(
        outer_kernel,
        in_specs=[SCALARS, WHOLE, ANY, ANY],
        out_specs=ANY,
        scratch_shapes=[
            pltpu.VMEM((K, M, D), BF16),
            pltpu.VMEM((K, M, D), BF16),
            pltpu.VMEM((D, D), BF16),
            pltpu.VMEM((NG, CARD + 1, PER, LANES), BF16),
            pltpu.VMEM((PER, LANES), F32),
            pltpu.SemaphoreType.DMA((2 * K,)),
            pltpu.SemaphoreType.DMA((K + 1,)),
        ],
        out_shape=jax.ShapeDtypeStruct((NG, CARD + 1, PER, LANES), BF16),
        compiler_params=vmem(56),
        cost_estimate=pl.CostEstimate(flops=2 * K * D * D * (M + M), bytes_accessed=4 << 20, transcendentals=0),
        name="outer",
    )(counts, fixed, x, grad)


def one_hot(found):
    return jnp.where(found, 1.0, 0.0).astype(BF16)


def line_of(part, z, away):
    line = (z + away * ((part & (WIDTH - 1)) >> 5) + NZ) & (NZ - 1)
    return (line << 1) + (part & 1)


def source_of(part):
    return ((part >> 1) & (E - 1)) + ((part >> 8) << 4)


HALF = 8
LINES = HALF // ROWS
BACK = (0, 4, 2, 6, 1, 5, 3, 7)


def stack_kernel(z, near, far, out):
    for n in range(NZ):
        source = near if n < NZ // 2 else far
        block = source[(n % (NZ // 2)) * PART : (n % (NZ // 2) + 1) * PART]
        line = (z[0] - BACK[n] + NZ) & (NZ - 1)
        half, place = line // LINES, (line & (LINES - 1)) * PART
        for part in range(2):
            out[half, pl.ds(pl.multiple_of(part * LINES * PART + place, PART), PART)] = block


def stack(z, near, far):
    return pl.pallas_call(
        stack_kernel,
        in_specs=[SCALARS, WHOLE, WHOLE],
        out_specs=WHOLE,
        out_shape=jax.ShapeDtypeStruct((2, WIDTH, D), BF16),
        compiler_params=vmem(STACK_MIB),
        cost_estimate=pl.CostEstimate(flops=0, bytes_accessed=6 * WIDTH * D, transcendentals=0),
        name="stack",
    )(z, near, far)


GROUPS = NG // GROUP
TALL = STEP * PER


def merge_kernel(message, rows, out, cards, weights, wide, held, ins, outs):
    fetch_cards = pltpu.make_async_copy(message.at[:, pl.ds(CARD, 1)], cards, ins.at[0])
    fetch_rows = [pltpu.make_async_copy(rows.at[h], weights.at[h], ins.at[1 + h]) for h in range(2)]

    def send(n):
        place = pl.ds(n * GROUP, GROUP)
        return pltpu.make_async_copy(held.at[place], out.at[place], outs.at[n])

    fetch_cards.start()
    for copy in fetch_rows:
        copy.start()
    system = row_of((NG * K, 1), 0)
    pick = one_hot(((system >> 2) << 4) + (system & (K - 1)) == row_of((1, NG * PER), 1))
    col = row_of((1, WIDTH), 1)
    source = ((col >> 1) & (E - 1)) + ((col >> 7) << 4)
    widen = one_hot(row_of((LANES, 1), 0) == source)
    place = (((col >> 5) & (LINES - 1)) << 1) + (col & 1)
    same = row_of((HALF, 1), 0) == place
    fetch_cards.wait()
    values = matmul(pick, cards[...].reshape(NG * PER, LANES), ((1,), (0,))).astype(BF16)
    wide[...] = matmul(values, widen, ((1,), (0,)))
    for copy in fetch_rows:
        copy.wait()
    for n in range(GROUPS):
        tall = jnp.where(same[None], wide[n * STEP : (n + 1) * STEP][:, None, :], 0.0)
        factor = tall.reshape(STEP * HALF, WIDTH).astype(BF16)
        halves = [matmul(factor, weights[h], ((1,), (0,))).reshape(STEP, HALF, D) for h in range(2)]
        merged = jnp.concatenate(halves, axis=1).astype(BF16)
        held[n * GROUP : (n + 1) * GROUP] = merged.reshape(GROUP, K, PER, D)
        send(n).start()
    for n in range(GROUPS):
        send(n).wait()


def merge(message, rows):
    return pl.pallas_call(
        merge_kernel,
        in_specs=[ANY, ANY],
        out_specs=ANY,
        scratch_shapes=[
            pltpu.VMEM((NG, 1, PER, LANES), BF16),
            pltpu.VMEM((2, WIDTH, D), BF16),
            pltpu.VMEM((NG * K, WIDTH), F32),
            pltpu.VMEM((NG, K, PER, D), BF16),
            pltpu.SemaphoreType.DMA((3,)),
            pltpu.SemaphoreType.DMA((GROUPS,)),
        ],
        out_shape=jax.ShapeDtypeStruct((NG, K, PER, D), BF16),
        compiler_params=vmem(MERGE_MIB),
        cost_estimate=pl.CostEstimate(flops=2 * NG * K * PER * WIDTH * D, bytes_accessed=3 << 20, transcendentals=0),
        name="merge",
    )(message, rows)


def mix_kernel(z, message, *refs):
    out, (held, total, low, ins, outs) = refs[:NZ], refs[NZ:]
    fetches = []
    for n in range(GROUPS):
        place = pl.ds(n * GROUP, GROUP)
        fetches.append(pltpu.make_async_copy(message.at[place], held.at[place], ins.at[n]))
        fetches[n].start()
    tall = row_of((1, TALL), 1)
    pick = one_hot(row_of((GROUP * PER, 1), 0) == (((tall >> 4) & (GROUP - 1)) << 4) + (tall >> 7))
    part = row_of((2 * WIDTH, 1), 0)
    widen = one_hot(source_of(part) == row_of((1, LANES), 1))
    same = line_of(part, z[0], 1) == (tall & (PER - 1))
    for n in range(GROUPS):
        fetches[n].wait()
        place = slice(n * GROUP, (n + 1) * GROUP)
        tiles = held[place, CARD].reshape(GROUP * PER, LANES)
        values = matmul(tiles, pick, ((0,), (0,))).astype(BF16)
        factor = jnp.where(same, matmul(widen, values, ((1,), (0,))), 0.0).astype(BF16)
        columns = []
        for tile in range(TILES):
            pieces = [held[place, k * TILES + tile].reshape(GROUP * PER, LANES) for k in range(K)]
            columns.append(jnp.concatenate(pieces, axis=0))
        both = matmul(factor, jnp.concatenate(columns, axis=1), ((1,), (0,)))
        sums = both[:WIDTH] + both[WIDTH:]
        total[...] = sums if n == 0 else total[...] + sums
    low[...] = total[...].astype(BF16)
    out[0][...] = total[:PART]
    sends = []
    for n in range(1, NZ):
        sends.append(pltpu.make_async_copy(low.at[pl.ds(n * PART, PART)], out[n], outs.at[n - 1]))
    for copy in sends:
        copy.start()
    for copy in sends:
        copy.wait()


def mix(z, message):
    return pl.pallas_call(
        mix_kernel,
        in_specs=[SCALARS, ANY],
        out_specs=[WHOLE] + [ANY] * (NZ - 1),
        scratch_shapes=[
            pltpu.VMEM((NG, CARD + 1, PER, LANES), BF16),
            pltpu.VMEM((WIDTH, D), F32),
            pltpu.VMEM((WIDTH, D), BF16),
            pltpu.SemaphoreType.DMA((GROUPS,)),
            pltpu.SemaphoreType.DMA((NZ - 1,)),
        ],
        out_shape=[jax.ShapeDtypeStruct((PART, D), F32)]
        + [jax.ShapeDtypeStruct((PART, D), BF16)] * (NZ - 1),
        compiler_params=vmem(MIX_MIB),
        cost_estimate=pl.CostEstimate(flops=4 * NG * K * PER * WIDTH * D, bytes_accessed=3 << 20, transcendentals=0),
        name="mix",
    )(z, message)


def total_kernel(own, *refs):
    *sums, out = refs
    total = own[...]
    for part in sums:
        total += part[...].astype(F32)
    for e in range(E):
        out[e] = total[ROWS * e : ROWS * (e + 1)]


def total(own, sums):
    return pl.pallas_call(
        total_kernel,
        out_shape=jax.ShapeDtypeStruct((E, ROWS, D), F32),
        compiler_params=vmem(8),
        cost_estimate=pl.CostEstimate(flops=WIDTH * D, bytes_accessed=5 * WIDTH * D, transcendentals=0),
        name="total",
    )(own, *sums)


def back_kernel(counts, grad, merged, out, pick, near, held, outs):
    def send(k):
        return pltpu.make_async_copy(held.at[k], out.at[k], outs.at[k])

    pick[...] = order()
    for k in range(K):
        masked = masked_of(grad[k], counts[k])
        near[k] = matmul(masked, merged[:, k].reshape(D, D), ((1,), (1,))).astype(BF16)
        if k == 1 or k == 3:
            for system in (k - 1, k):
                held[system] = matmul(near[system], pick[...], ((1,), (0,))).astype(BF16)
                send(system).start()
    for k in range(K):
        send(k).wait()


def back(counts, grad, merged):
    return pl.pallas_call(
        back_kernel,
        in_specs=[SCALARS, WHOLE, WHOLE],
        out_specs=ANY,
        scratch_shapes=[
            pltpu.VMEM((D, D), BF16),
            pltpu.VMEM((K, M, D), BF16),
            pltpu.VMEM((K, M, D), BF16),
            pltpu.SemaphoreType.DMA((K,)),
        ],
        out_shape=jax.ShapeDtypeStruct((K, M, D), BF16),
        compiler_params=vmem(BACK_MIB),
        cost_estimate=pl.CostEstimate(flops=4 * K * M * D * D, bytes_accessed=4 << 20, transcendentals=0),
        name="back",
    )(counts, grad, merged)


def swap(array, axes):
    return lax.all_to_all(array, axes, 0, 0, tiled=True)


def along_z(array, by):
    return lax.ppermute(array, "z", [(i, (i + by) % NZ) for i in range(NZ)])


def shards(inputs, out_grad, coeff_fixed, atom_counts, experts):
    z = lax.axis_index("z").astype(jnp.int32).reshape(1)
    message = swap(outer(atom_counts, coeff_fixed, inputs, out_grad), PLANE)
    own = experts.reshape(PART, D)
    near = jnp.concatenate([own, along_z(own, 4)])
    near = jnp.concatenate([near, along_z(near, 2)])
    rows = stack(z, near, along_z(near, 1))
    merged = swap(merge(message, rows), PLANE)
    mixed = mix(z, message)
    sums = [along_z(mixed[n], n) for n in range(1, NZ)]
    return back(atom_counts, out_grad, merged), total(mixed[0], sums)


def solution(mesh):
    split = Mesh(mesh.devices.reshape([size for _, size in AXES]), NAMES)
    placed = (
        P(NAMES, None, None),
        P(NAMES, None, None),
        P(NAMES, None),
        P(NAMES),
        P(None, NAMES, None),
    )
    return jax.shard_map(
        shards,
        mesh=split,
        in_specs=placed,
        out_specs=(P(NAMES, None, None), P(None, NAMES, None)),
        check_vma=False,
    )
```
